512 devices in a mesh: blk: 64 (over x, y_lo, z), grp: 8 (over y_hi, core).
Axes of the slice: x: 4, y: 8 (y_hi: 4, y_lo: 2; y = y_hi * 2 + y_lo), z: 8, core: 2. Of those that a mesh axis runs over, the one named last changes fastest.
Arguments:
- user_factors: float32 [524288, 256], P(('grp', 'blk')), parts along dimension 0, may hold values from -1.5 to 1.5
- item_factors: float32 [262144, 256], P(('grp', 'blk')), parts along dimension 0, may hold values from -1.5 to 1.5
- ratings: bfloat16 [24576, 128, 128], P(('grp', 'blk')), parts along dimension 0, may hold values from -4.1 to 4.1, as said below
- tile_lists: int32 [2048, 2, 12], P(('grp', 'blk')), parts along dimension 0, may hold values from 0 to 3, as said below
- tile_counts: int32 [2048], P(('grp', 'blk')), parts along dimension 0, may hold values from 2 to 12, as said below
Outputs:
- new_users: float32 [524288, 256], P(('grp', 'blk')), parts along dimension 0
- new_items: float32 [262144, 256], P(('grp', 'blk')), parts along dimension 0
The draws below stay inside these ranges and needn't reach their ends.
There are 8 independent parts, one for each index of `grp`. The reference program is written for one: setup_inputs(seed, part) draws one part's arguments, and reference() takes and returns one part's arrays. A program takes and returns all parts, laid end to end along the dimension named above; each array names one. Nothing has to cross between parts.
Inputs may be any that keep to these rules, and one draw needn't show every extreme that they name: `ratings`: zero marks a missing rating; every other entry lies at least 0.1 away from zero. `tile_lists`: the 12 slots of one list name distinct tile positions; row 0 is below 4 and row 1 below 4; slots at or after the list's count hold arbitrary positions and tiles. `tile_counts`: some list of every draw is full.
All inputs are finite; a program needn't handle non-finite values.
Results may differ from the reference program's by a relative error of at most 0.0003.
Values may be sent and summed in bfloat16 or wider, within the bound.
No kernel may reach another device: no remote copies, remote signals or barrier semaphores. Data moves between devices by JAX's collectives and lax.ppermute only.
A program may use at most 64 MiB of HBM per device.

```python
import jax
import jax.numpy as jnp
from jax import lax

R = 256
TILE = 128
BLOCK = 512
BATCH_USERS = 512
BATCHES = 2
VISITS = 2
SLOTS = 12
USERS_DEV = 1024
USERS = 65536
ITEMS = 32768
LISTS = 256
RATE_TILES = 3072
PAIRS = 16
N_BLK = 64


def draw_ratings(key, part):
    key = jax.random.fold_in(key, 13)
    key_keep, key_value = jax.random.split(key, 2)
    shape = (RATE_TILES, TILE, TILE)
    keep = jax.random.bernoulli(key_keep, 2.0 / 3.0, shape)
    normal_part = jax.random.normal(key_value, shape, jnp.float32)
    magnitude = 0.1 + jnp.minimum(jnp.abs(normal_part), 4.0)
    sign_part = jnp.where(normal_part >= 0, 1.0, -1.0)
    return jnp.where(keep, sign_part * magnitude, 0.0).astype(jnp.bfloat16)


def draw_tile_lists(key, part):
    key = jax.random.fold_in(key, 11)
    keys = jax.random.split(key, LISTS)
    orders = jax.vmap(lambda single: jax.random.permutation(single, PAIRS))(keys)[:, :SLOTS]
    per_row = BLOCK // TILE
    return jnp.stack([orders // per_row, orders % per_row], axis=1).astype(jnp.int32)


def draw_tile_counts(key, part):
    key = jax.random.fold_in(key, 12)
    key_counts, key_pick = jax.random.split(key)
    counts = jax.random.randint(key_counts, (LISTS,), 2, SLOTS + 1)
    chosen = jax.random.randint(key_pick, (), 0, LISTS)
    counts = counts.at[chosen].set(SLOTS)
    counts = counts.at[(chosen + 1) % LISTS].set(2)
    return counts.astype(jnp.int32)


def shard_levels(key, dims, shards, low, high):
    gain, own = 1.0, jax.random.fold_in(key, 6)
    for position, parts in shards:
        steps = jnp.exp(jax.random.uniform(jax.random.fold_in(own, position), (parts,), jnp.float32, low / len(shards), high / len(shards)))
        gain = gain * jnp.repeat(steps, dims[position] // parts).reshape([-1 if axis == position else 1 for axis in range(len(dims))])
    return gain


def noise(stream_key, dims, spread, reach, cuts=(), held_as=jnp.bfloat16):
    array = jax.random.normal(stream_key, dims, jnp.float32) * spread
    if len(cuts) > 0:
        array = shard_levels(stream_key, dims, cuts, -0.22, 0.18) * array
    return jnp.clip(array, min=-reach, max=reach).astype(held_as)


def setup_inputs(seed: int = 0, part: int = 0) -> dict:
    seeds = jax.random.split(jax.random.key(seed), 6)
    part_keys = jax.random.split(jax.random.fold_in(seeds[5], part), 6)
    return {
        "user_factors": noise(part_keys[0], (USERS, R), 0.25, 1.5, ((0, 64),), jnp.float32),
        "item_factors": noise(part_keys[1], (ITEMS, R), 0.25, 1.5, ((0, 64),), jnp.float32),
        "ratings": draw_ratings(jax.random.fold_in(jax.random.fold_in(seeds[5], part), 71), part),
        "tile_lists": draw_tile_lists(jax.random.fold_in(jax.random.fold_in(seeds[5], part), 71), part),
        "tile_counts": draw_tile_counts(jax.random.fold_in(jax.random.fold_in(seeds[5], part), 71), part),
    }


LEARN = 0.02
DECAY = 0.05


def batch_step(user_rows, item_block, tile_block, tile_pairs, live_count):
    width = user_rows.shape[1]
    user_tiles = user_rows.reshape(-1, TILE, width)
    item_tiles = item_block.reshape(-1, TILE, width)
    grad_users = jnp.zeros_like(user_tiles)
    grad_items = jnp.zeros_like(item_tiles)
    for slot_index in range(SLOTS):
        active = (slot_index < live_count).astype(jnp.float32)
        row_pos = tile_pairs[0, slot_index]
        col_pos = tile_pairs[1, slot_index]
        user_tile = user_tiles[row_pos]
        item_tile = item_tiles[col_pos]
        observed = tile_block[slot_index].astype(jnp.float32)
        predicted = jnp.dot(user_tile, item_tile.T, precision=lax.Precision.HIGHEST, preferred_element_type=jnp.float32)
        residue = jnp.where(observed != 0, predicted - observed, 0.0) * active
        grad_users = grad_users.at[row_pos].add(jnp.dot(residue, item_tile, precision=lax.Precision.HIGHEST, preferred_element_type=jnp.float32))
        grad_items = grad_items.at[col_pos].add(jnp.dot(residue.T, user_tile, precision=lax.Precision.HIGHEST, preferred_element_type=jnp.float32))
    new_rows = user_rows - LEARN * (grad_users.reshape(user_rows.shape) + DECAY * user_rows)
    new_block = item_block - LEARN * (grad_items.reshape(item_block.shape) + DECAY * item_block)
    return new_rows, new_block


def one_visit(bundle):
    user_rows, item_block, tile_block, tile_pairs, live_counts = bundle
    pieces = []
    for batch_index in range(BATCHES):
        part = user_rows[batch_index * BATCH_USERS:(batch_index + 1) * BATCH_USERS]
        tiles_now = tile_block[batch_index * SLOTS:(batch_index + 1) * SLOTS]
        part, item_block = batch_step(part, item_block, tiles_now, tile_pairs[batch_index], live_counts[batch_index])
        pieces.append(part)
    return jnp.concatenate(pieces, axis=0), item_block


def reference(user_factors, item_factors, ratings, tile_lists, tile_counts):
    stripes = user_factors.reshape(N_BLK, USERS_DEV, R)
    blocks = item_factors.reshape(N_BLK, BLOCK, R)
    tiles_all = ratings.reshape(N_BLK, VISITS, BATCHES * SLOTS, TILE, TILE)
    pairs_all = tile_lists.reshape(N_BLK, VISITS, BATCHES, 2, SLOTS)
    counts_all = tile_counts.reshape(N_BLK, VISITS, BATCHES)
    for visit_index in range(VISITS):
        stripes, blocks = lax.map(one_visit, (stripes, blocks, tiles_all[:, visit_index], pairs_all[:, visit_index], counts_all[:, visit_index]))
        if visit_index + 1 < VISITS:
            blocks = jnp.roll(blocks, 1, axis=0)
    blocks = jnp.roll(blocks, -(VISITS - 1), axis=0)
    return stripes.reshape(USERS, R), blocks.reshape(ITEMS, R)
```

```python
import jax
import jax.numpy as jnp
from jax import lax
from jax.experimental import pallas as pl
from jax.experimental.pallas import tpu as pltpu
from jax.sharding import PartitionSpec as P

TILE = 128
BATCHES = 2
VISITS = 2
SLOTS = 12
SIDE = 4
PLACES = SIDE * SIDE
ROWS = SIDE * TILE
RANK = 256
HALVES = 2
HALF = ROWS // HALVES
EXTRA = 16
CODED = HALF + EXTRA
LISTED = BATCHES * SLOTS

LEARN = 0.02
DECAY = 0.05
TOP = 32766.0
F32 = jnp.float32
BF16 = jnp.bfloat16


def passed_along(value, axis, steps):
    count = lax.axis_size(axis)
    pairs = [(source, (source + steps) % count) for source in range(count)]
    return lax.ppermute(value, axis, pairs)


def split(value):
    high = value.astype(BF16)
    low = (value - high.astype(F32)).astype(BF16)
    return high, low


def product(left, right, dims):
    def dot(a, b):
        return lax.dot_general(a, b, (dims, ((), ())), preferred_element_type=F32)

    return dot(left[0], right[0]) + (dot(left[1], right[0]) + dot(left[0], right[1]))


def encode(block):
    peak = jnp.maximum(jnp.max(jnp.abs(block), axis=0, keepdims=True), 1e-30)
    power = jnp.ceil(jnp.log2(peak))
    unit = jnp.exp2(power - 8.0)
    units = jnp.ceil(peak / unit)
    coded = jnp.round(block * (TOP / (units * unit))).astype(jnp.int32)
    row = lax.broadcasted_iota(jnp.int32, (EXTRA, RANK), 0)
    scale = jnp.where(
        row == 0, power.astype(jnp.int32), jnp.where(row == 1, units.astype(jnp.int32), 0)
    )
    return coded.astype(jnp.int16), scale.astype(jnp.int16)


def decode(coded, scale):
    scale = scale.astype(jnp.int32).astype(F32)
    step = scale[1:2] * jnp.exp2(scale[0:1] - 8.0) * (1.0 / TOP)
    return coded.astype(jnp.int32).astype(F32) * step


def visit_kernel(
    visit, lists_in, counts_in, users_in, items_in, ratings_in, users_out, items_out,
    users, items, tiles, lists, counts, where, users_high, users_low, grads, sems,
):
    user_copies, tile_copies, out_copies = [], [], []
    list_copy = pltpu.make_async_copy(lists_in, lists, sems.at[7])
    count_copy = pltpu.make_async_copy(counts_in, counts, sems.at[8])
    list_copy.start()
    count_copy.start()
    if visit == 0:
        item_copy = pltpu.make_async_copy(items_in, items, sems.at[4])
        item_copy.start()
        old_users, new_users = users, users_out
    else:
        old_users, new_users = users_in, users
    for batch in range(BATCHES):
        rows = pl.ds(batch * ROWS, ROWS)
        if visit == 0:
            user_copies.append(
                pltpu.make_async_copy(users_in.at[rows], users.at[rows], sems.at[batch])
            )
            user_copies[-1].start()
        first = visit * LISTED + batch * SLOTS
        tile_copies.append(
            pltpu.make_async_copy(
                ratings_in.at[pl.ds(first, SLOTS)],
                tiles.at[pl.ds(batch * SLOTS, SLOTS)],
                sems.at[2 + batch],
            )
        )
        tile_copies[-1].start()
    tiles[LISTED] = jnp.zeros((TILE, TILE), BF16)
    list_copy.wait()
    count_copy.wait()
    for batch in range(BATCHES):
        entry = visit * BATCHES + batch
        for place in range(PLACES):
            where[batch * PLACES + place] = LISTED

        def note(slot, carry):
            place = lists[entry, 0, slot] * SIDE + lists[entry, 1, slot]
            where[batch * PLACES + place] = batch * SLOTS + slot
            return carry

        lax.fori_loop(0, counts[entry], note, 0)

    def residue(predicted, batch, half):
        highs, lows = [], []
        for user_tile in range(SIDE):
            high_row, low_row = [], []
            for item_tile in range(SIDE // HALVES):
                place = user_tile * SIDE + half * (SIDE // HALVES) + item_tile
                observed = tiles[where[batch * PLACES + place]].astype(F32)
                part = predicted[
                    user_tile * TILE : (user_tile + 1) * TILE,
                    item_tile * TILE : (item_tile + 1) * TILE,
                ]
                high, low = split(jnp.where(observed != 0, part - observed, 0.0))
                high_row.append(high)
                low_row.append(low)
            highs.append(jnp.concatenate(high_row, axis=1))
            lows.append(jnp.concatenate(low_row, axis=1))
        return jnp.concatenate(highs, axis=0), jnp.concatenate(lows, axis=0)

    for half in range(HALVES):
        span = pl.ds(half * HALF, HALF)
        if visit == 0:
            if half == 0:
                item_copy.wait()
            block = items[span]
        else:
            block = decode(items_in[half, :HALF], items_in[half, HALF:])
        for batch in range(BATCHES):
            rows = pl.ds(batch * ROWS, ROWS)
            if half == 0:
                if visit == 0:
                    user_copies[batch].wait()
                high, low = split(old_users[rows])
                users_high[rows] = high
                users_low[rows] = low
            batch_users = (users_high[rows], users_low[rows])
            block_parts = split(block)
            predicted = product(batch_users, block_parts, ((1,), (1,)))
            if half == 0:
                tile_copies[batch].wait()
            left = residue(predicted, batch, half)
            grad_users = product(left, block_parts, ((1,), (0,)))
            if half == 0:
                grads[rows] = grad_users
            else:
                old = old_users[rows]
                new_users[rows] = old - LEARN * ((grads[rows] + grad_users) + DECAY * old)
                if visit == 1:
                    out_copies.append(
                        pltpu.make_async_copy(
                            users.at[rows], users_out.at[rows], sems.at[5 + batch]
                        )
                    )
                    out_copies[-1].start()
            grad_items = product(left, batch_users, ((0,), (0,)))
            block = block - LEARN * (grad_items + DECAY * block)
        coded, scale = encode(block)
        items_out[half, :HALF] = coded
        items_out[half, HALF:] = scale
    for copy in out_copies:
        copy.wait()


def held(value):
    return pltpu.with_memory_space_constraint(value, pltpu.HBM)


def visit_call(visit, lists, counts, users, items, ratings):
    spec_hbm = pl.BlockSpec(memory_space=pltpu.HBM)
    spec_vmem = pl.BlockSpec(memory_space=pltpu.VMEM)

    def kernel(*refs):
        visit_kernel(visit, *refs)

    return pl.pallas_call(
        kernel,
        out_shape=(
            jax.ShapeDtypeStruct((BATCHES * ROWS, RANK), F32),
            jax.ShapeDtypeStruct((HALVES, CODED, RANK), jnp.int16),
        ),
        in_specs=[
            spec_hbm,
            spec_hbm,
            spec_hbm if visit == 0 else spec_vmem,
            spec_hbm if visit == 0 else spec_vmem,
            spec_hbm,
        ],
        out_specs=(spec_vmem if visit == 0 else spec_hbm, spec_vmem),
        scratch_shapes=[
            pltpu.VMEM((BATCHES * ROWS, RANK), F32),
            pltpu.VMEM((ROWS, RANK), F32),
            pltpu.VMEM((LISTED + 1, TILE, TILE), BF16),
            pltpu.SMEM((VISITS * BATCHES, 2, SLOTS), jnp.int32),
            pltpu.SMEM((VISITS * BATCHES,), jnp.int32),
            pltpu.SMEM((BATCHES * PLACES,), jnp.int32),
            pltpu.VMEM((BATCHES * ROWS, RANK), BF16),
            pltpu.VMEM((BATCHES * ROWS, RANK), BF16),
            pltpu.VMEM((BATCHES * ROWS, RANK), F32),
            pltpu.SemaphoreType.DMA((9,)),
        ],
        compiler_params=pltpu.CompilerParams(vmem_limit_bytes=40 * 1024 * 1024),
        name=f"visit{visit}",
    )(
        held(lists),
        held(counts),
        held(users) if visit == 0 else users,
        held(items) if visit == 0 else items,
        held(ratings),
    )


def decode_kernel(coded, items):
    for half in range(HALVES):
        items[half * HALF : (half + 1) * HALF] = decode(coded[half, :HALF], coded[half, HALF:])


def decode_call(coded):
    spec_vmem = pl.BlockSpec(memory_space=pltpu.VMEM)
    return pl.pallas_call(
        decode_kernel,
        out_shape=jax.ShapeDtypeStruct((ROWS, RANK), F32),
        in_specs=[spec_vmem],
        out_specs=spec_vmem,
        compiler_params=pltpu.CompilerParams(vmem_limit_bytes=8 * 1024 * 1024),
        name="unpack",
    )(coded)


def on_device(user_factors, item_factors, ratings, tile_lists, tile_counts):
    users, coded = visit_call(0, tile_lists, tile_counts, user_factors, item_factors, ratings)
    arrived = passed_along(coded, "blk", 1)
    users, coded = visit_call(1, tile_lists, tile_counts, users, arrived, ratings)
    items = decode_call(passed_along(coded, "blk", -1))
    return (users, items)


def solution(mesh):
    in_specs = (
        P(("grp", "blk"), None),
        P(("grp", "blk"), None),
        P(("grp", "blk"), None, None),
        P(("grp", "blk"), None, None),
        P(("grp", "blk")),
    )
    out_specs = (P(("grp", "blk"), None), P(("grp", "blk"), None))
    return jax.shard_map(
        on_device, mesh=mesh, in_specs=in_specs, out_specs=out_specs, check_vma=False
    )
```

```python
import jax
import jax.numpy as jnp
from jax import lax
from jax.experimental import pallas as pl
from jax.experimental.pallas import tpu as pltpu
from jax.sharding import PartitionSpec as P

TILE = 128
BATCHES = 2
VISITS = 2
SLOTS = 12
SIDE = 4
PLACES = SIDE * SIDE
ROWS = SIDE * TILE
RANK = 256
HALVES = 2
HALF = ROWS // HALVES
EXTRA = 16
CODED = HALF + EXTRA
ENTRIES = VISITS * BATCHES
NONE = ENTRIES * SLOTS

LEARN = 0.02
DECAY = 0.05
TOP = 32766.0
F32 = jnp.float32
BF16 = jnp.bfloat16


def passed_along(value, axis, steps):
    count = lax.axis_size(axis)
    pairs = [(source, (source + steps) % count) for source in range(count)]
    return lax.ppermute(value, axis, pairs)


def split(value):
    high = value.astype(BF16)
    low = (value - high.astype(F32)).astype(BF16)
    return high, low


def dot(left, right, dims):
    return lax.dot_general(left, right, (dims, ((), ())), preferred_element_type=F32)


def product(left, right, dims):
    (left_dim,), (right_dim,) = dims
    wide = jnp.concatenate([left[0], left[1], left[0]], axis=left_dim)
    tall = jnp.concatenate([right[0], right[0], right[1]], axis=right_dim)
    return dot(wide, tall, dims)


def encode(block):
    peak = jnp.maximum(jnp.max(jnp.abs(block), axis=0, keepdims=True), 1e-30)
    power = jnp.ceil(jnp.log2(peak))
    unit = jnp.exp2(power - 8.0)
    units = jnp.ceil(peak / unit)
    coded = jnp.round(block * (TOP / (units * unit))).astype(jnp.int32)
    row = lax.broadcasted_iota(jnp.int32, (EXTRA, RANK), 0)
    scale = jnp.where(
        row == 0, power.astype(jnp.int32), jnp.where(row == 1, units.astype(jnp.int32), 0)
    )
    return coded.astype(jnp.int16), scale.astype(jnp.int16)


def decode(coded, scale):
    scale = scale.astype(jnp.int32).astype(F32)
    step = scale[1:2] * jnp.exp2(scale[0:1] - 8.0) * (1.0 / TOP)
    return coded.astype(jnp.int32).astype(F32) * step


CHUNK = 512
CHUNKS = ROWS // CHUNK


def visit_batch(observed_tile, users_of, block, store_users):
    block_parts = split(block)
    grad_items = jnp.zeros((ROWS, RANK), F32)
    for chunk in range(CHUNKS):
        old = users_of(chunk)
        parts = split(old)
        predicted = product(parts, block_parts, ((1,), (1,)))
        highs, lows = [], []
        for user_tile in range(CHUNK // TILE):
            high_row, low_row = [], []
            for item_tile in range(SIDE):
                observed = observed_tile(chunk * (CHUNK // TILE) + user_tile, item_tile)
                observed = observed.astype(F32)
                part = predicted[
                    user_tile * TILE : (user_tile + 1) * TILE,
                    item_tile * TILE : (item_tile + 1) * TILE,
                ]
                high, low = split(jnp.where(observed != 0, part - observed, 0.0))
                high_row.append(high)
                low_row.append(low)
            highs.append(jnp.concatenate(high_row, axis=1))
            lows.append(jnp.concatenate(low_row, axis=1))
        left = (jnp.concatenate(highs, axis=0), jnp.concatenate(lows, axis=0))
        grad_users = product(left, block_parts, ((1,), (0,)))
        store_users(chunk, old - LEARN * (grad_users + DECAY * old))
        grad_items = grad_items + product(left, parts, ((0,), (0,)))
    return block - LEARN * (grad_items + DECAY * block)


def chunk_rows(batch, chunk):
    return pl.ds(batch * ROWS + chunk * CHUNK, CHUNK)


def store_coded(block, items_out):
    for half in range(HALVES):
        coded, scale = encode(block[half * HALF : (half + 1) * HALF])
        items_out[half, :HALF] = coded
        items_out[half, HALF:] = scale


def first_kernel(
    lists_in, counts_in, users_in, items_in, ratings_in, users_out, items_out, later_out,
    users, items, tiles, lists, counts, where, sems,
):
    def fetch(source, target, sem):
        return pltpu.make_async_copy(source, target, sems.at[sem])

    item_copy = fetch(items_in, items, 0)
    user_copies = [
        fetch(users_in.at[chunk_rows(batch, chunk)], users.at[chunk_rows(batch, chunk)], 8 + batch * CHUNKS + chunk)
        for batch in range(BATCHES)
        for chunk in range(CHUNKS)
    ]
    tile_copies = [
        fetch(ratings_in.at[pl.ds(entry * SLOTS, SLOTS)], tiles.at[pl.ds(entry * SLOTS, SLOTS)], 1 + entry)
        for entry in range(ENTRIES)
    ]
    list_copy = fetch(lists_in, lists, 5)
    count_copy = fetch(counts_in, counts, 6)
    list_copy.start()
    count_copy.start()
    item_copy.start()
    for batch in range(BATCHES):
        for chunk in range(CHUNKS):
            user_copies[batch * CHUNKS + chunk].start()
        tile_copies[batch].start()
    for entry in range(BATCHES, ENTRIES):
        tile_copies[entry].start()
    tiles[NONE] = jnp.zeros((TILE, TILE), BF16)
    list_copy.wait()
    count_copy.wait()
    for entry in range(ENTRIES):
        for place in range(PLACES):
            where[entry * PLACES + place] = NONE

        def note(slot, carry):
            place = lists[entry, 0, slot] * SIDE + lists[entry, 1, slot]
            where[entry * PLACES + place] = entry * SLOTS + slot
            return carry

        lax.fori_loop(0, counts[entry], note, 0)
    item_copy.wait()
    block = items[...]
    for batch in range(BATCHES):
        for chunk in range(CHUNKS):
            user_copies[batch * CHUNKS + chunk].wait()
        tile_copies[batch].wait()

        def store_users(chunk, rows):
            users_out[chunk_rows(batch, chunk)] = rows

        block = visit_batch(
            lambda row, column: tiles[where[batch * PLACES + row * SIDE + column]],
            lambda chunk: users[chunk_rows(batch, chunk)],
            block,
            store_users,
        )
    store_coded(block, items_out)
    for entry in range(BATCHES, ENTRIES):
        tile_copies[entry].wait()
        for place in range(PLACES):
            later_out[(entry - BATCHES) * PLACES + place] = tiles[where[entry * PLACES + place]]


def second_kernel(users_in, items_in, later_in, users_out, items_out, users, sems):
    block = jnp.concatenate(
        [decode(items_in[half, :HALF], items_in[half, HALF:]) for half in range(HALVES)], axis=0
    )
    copies = []
    for batch in range(BATCHES):

        def store_users(chunk, rows):
            users[chunk_rows(batch, chunk)] = rows
            copies.append(
                pltpu.make_async_copy(
                    users.at[chunk_rows(batch, chunk)],
                    users_out.at[chunk_rows(batch, chunk)],
                    sems.at[len(copies)],
                )
            )
            copies[-1].start()

        block = visit_batch(
            lambda row, column: later_in[batch * PLACES + row * SIDE + column],
            lambda chunk: users_in[chunk_rows(batch, chunk)],
            block,
            store_users,
        )
    store_coded(block, items_out)
    for copy in copies:
        copy.wait()


def held(value):
    return pltpu.with_memory_space_constraint(value, pltpu.HBM)


SPEC_HBM = pl.BlockSpec(memory_space=pltpu.HBM)
SPEC_VMEM = pl.BlockSpec(memory_space=pltpu.VMEM)
PARAMS = pltpu.CompilerParams(vmem_limit_bytes=40 * 1024 * 1024)
CODED_SHAPE = jax.ShapeDtypeStruct((HALVES, CODED, RANK), jnp.int16)
USERS_SHAPE = jax.ShapeDtypeStruct((BATCHES * ROWS, RANK), F32)


def first_call(lists, counts, users, items, ratings):
    return pl.pallas_call(
        first_kernel,
        out_shape=(
            USERS_SHAPE,
            CODED_SHAPE,
            jax.ShapeDtypeStruct((BATCHES * PLACES, TILE, TILE), BF16),
        ),
        in_specs=[SPEC_HBM] * 5,
        out_specs=(SPEC_VMEM,) * 3,
        scratch_shapes=[
            pltpu.VMEM((BATCHES * ROWS, RANK), F32),
            pltpu.VMEM((ROWS, RANK), F32),
            pltpu.VMEM((NONE + 1, TILE, TILE), BF16),
            pltpu.SMEM((ENTRIES, 2, SLOTS), jnp.int32),
            pltpu.SMEM((ENTRIES,), jnp.int32),
            pltpu.SMEM((ENTRIES * PLACES,), jnp.int32),
            pltpu.SemaphoreType.DMA((8 + BATCHES * CHUNKS,)),
        ],
        compiler_params=PARAMS,
        name="first_visit",
    )(held(lists), held(counts), held(users), held(items), held(ratings))


def second_call(users, items, later):
    return pl.pallas_call(
        second_kernel,
        out_shape=(USERS_SHAPE, CODED_SHAPE),
        in_specs=[SPEC_VMEM] * 3,
        out_specs=(SPEC_HBM, SPEC_VMEM),
        scratch_shapes=[
            pltpu.VMEM((BATCHES * ROWS, RANK), F32),
            pltpu.SemaphoreType.DMA((BATCHES * CHUNKS,)),
        ],
        compiler_params=PARAMS,
        name="second_visit",
    )(users, items, later)


def decode_kernel(coded, items):
    for half in range(HALVES):
        items[half * HALF : (half + 1) * HALF] = decode(coded[half, :HALF], coded[half, HALF:])


def decode_call(coded):
    spec_vmem = pl.BlockSpec(memory_space=pltpu.VMEM)
    return pl.pallas_call(
        decode_kernel,
        out_shape=jax.ShapeDtypeStruct((ROWS, RANK), F32),
        in_specs=[spec_vmem],
        out_specs=spec_vmem,
        compiler_params=pltpu.CompilerParams(vmem_limit_bytes=8 * 1024 * 1024),
        name="unpack",
    )(coded)


def on_device(user_factors, item_factors, ratings, tile_lists, tile_counts):
    users, coded, later = first_call(
        tile_lists, tile_counts, user_factors, item_factors, ratings
    )
    users, coded = second_call(users, passed_along(coded, "blk", 1), later)
    items = decode_call(passed_along(coded, "blk", -1))
    return (users, items)


def solution(mesh):
    in_specs = (
        P(("grp", "blk"), None),
        P(("grp", "blk"), None),
        P(("grp", "blk"), None, None),
        P(("grp", "blk"), None, None),
        P(("grp", "blk")),
    )
    out_specs = (P(("grp", "blk"), None), P(("grp", "blk"), None))
    return jax.shard_map(
        on_device, mesh=mesh, in_specs=in_specs, out_specs=out_specs, check_vma=False
    )
```

```python
import jax
import jax.numpy as jnp
from jax import lax
from jax.experimental import pallas as pl
from jax.experimental.pallas import tpu as pltpu
from jax.sharding import PartitionSpec as P

TILE = 128
BATCHES = 2
VISITS = 2
SLOTS = 12
SIDE = 4
PLACES = SIDE * SIDE
ROWS = SIDE * TILE
RANK = 256
HALVES = 2
HALF = ROWS // HALVES
EXTRA = 16
CODED = HALF + EXTRA
ENTRIES = VISITS * BATCHES
LISTED = BATCHES * SLOTS

LEARN = 0.02
DECAY = 0.05
TOP = 32766.0
F32 = jnp.float32
BF16 = jnp.bfloat16


def passed_along(value, axis, steps):
    count = lax.axis_size(axis)
    pairs = [(source, (source + steps) % count) for source in range(count)]
    return lax.ppermute(value, axis, pairs)


def split(value):
    high = value.astype(BF16)
    low = (value - high.astype(F32)).astype(BF16)
    return high, low


def dot(left, right, dims):
    return lax.dot_general(left, right, (dims, ((), ())), preferred_element_type=F32)


def product(left, right, dims):
    (left_dim,), (right_dim,) = dims
    wide = jnp.concatenate([left[0], left[1], left[0]], axis=left_dim)
    tall = jnp.concatenate([right[0], right[0], right[1]], axis=right_dim)
    return dot(wide, tall, dims)


def encode(block):
    peak = jnp.maximum(jnp.max(jnp.abs(block), axis=0, keepdims=True), 1e-30)
    power = jnp.ceil(jnp.log2(peak))
    unit = jnp.exp2(power - 8.0)
    units = jnp.ceil(peak / unit)
    coded = jnp.round(block * (TOP / (units * unit))).astype(jnp.int32)
    row = lax.broadcasted_iota(jnp.int32, (EXTRA, RANK), 0)
    scale = jnp.where(
        row == 0, power.astype(jnp.int32), jnp.where(row == 1, units.astype(jnp.int32), 0)
    )
    return coded.astype(jnp.int16), scale.astype(jnp.int16)


def decode(coded, scale):
    scale = scale.astype(jnp.int32).astype(F32)
    step = scale[1:2] * jnp.exp2(scale[0:1] - 8.0) * (1.0 / TOP)
    return coded.astype(jnp.int32).astype(F32) * step


def batch_rows(batch):
    return pl.ds(batch * ROWS, ROWS)


ORDER = "P00 P10 R00 R10 G00 G10 P01 P11 R01 R11 G01 G11"


def block_steps(observed_tile, users_of, halves, residues_out, blocks_out, before=None):
    parts, predicted, residues = {}, {}, {}
    columns = SIDE // HALVES
    for item in ORDER.split():
        kind, half, batch = item[0], int(item[1]), int(item[2])
        span = pl.ds(half * HALF, HALF)
        if before is not None:
            before(kind, half, batch)
        if kind == "P":
            parts[half] = split(halves[half])
            for which in range(2):
                blocks_out[batch, which, span] = parts[half][which]
            predicted[half] = product(users_of(batch), parts[half], ((1,), (1,)))
        elif kind == "R":
            highs, lows = [], []
            for row in range(SIDE):
                high_row, low_row = [], []
                for column in range(columns):
                    observed = observed_tile(batch, row * SIDE + half * columns + column)
                    observed = observed.astype(F32)
                    part = predicted[half][
                        row * TILE : (row + 1) * TILE, column * TILE : (column + 1) * TILE
                    ]
                    high, low = split(jnp.where(observed != 0, part - observed, 0.0))
                    high_row.append(high)
                    low_row.append(low)
                highs.append(jnp.concatenate(high_row, axis=1))
                lows.append(jnp.concatenate(low_row, axis=1))
            residues[half] = (jnp.concatenate(highs, axis=0), jnp.concatenate(lows, axis=0))
            for which in range(2):
                residues_out[batch, which, :, span] = residues[half][which]
        else:
            grad_items = product(residues[half], users_of(batch), ((0,), (0,)))
            halves[half] = halves[half] - LEARN * (grad_items + DECAY * halves[half])


def users_step(old, residues, blocks, batch):
    grad_users = product(
        (residues[batch, 0], residues[batch, 1]), (blocks[batch, 0], blocks[batch, 1]), ((1,), (0,))
    )
    return old - LEARN * (grad_users + DECAY * old)


def store_coded(halves, items_out):
    for half in range(HALVES):
        coded, scale = encode(halves[half])
        items_out[half, :HALF] = coded
        items_out[half, HALF:] = scale


def place_slots(where, lists, counts, visit):
    for batch in range(BATCHES):
        entry = visit * BATCHES + batch
        base = batch * (PLACES + 1)
        count = counts[entry]
        for place in range(PLACES):
            where[base + place] = LISTED
        for slot in range(SLOTS):
            row = jnp.clip(lists[entry, 0, slot], 0, SIDE - 1)
            column = jnp.clip(lists[entry, 1, slot], 0, SIDE - 1)
            live = slot < count
            where[base + jnp.where(live, row * SIDE + column, PLACES)] = batch * SLOTS + slot


def fetch_lists(lists_in, counts_in, lists, counts, sems):
    copies = (
        pltpu.make_async_copy(lists_in, lists, sems.at[0]),
        pltpu.make_async_copy(counts_in, counts, sems.at[1]),
    )
    for copy in copies:
        copy.start()
    return copies


def fetch_tiles(ratings_in, tiles, visit, batch, sem):
    first = (visit * BATCHES + batch) * SLOTS
    copy = pltpu.make_async_copy(
        ratings_in.at[pl.ds(first, SLOTS)], tiles.at[pl.ds(batch * SLOTS, SLOTS)], sem
    )
    copy.start()
    return copy


def first_block_kernel(
    lists_in, counts_in, users_in, items_in, ratings_in,
    users, items_out, residues_out, blocks_out,
    items, tiles, lists, counts, where, sems,
):
    list_copies = fetch_lists(lists_in, counts_in, lists, counts, sems)
    copies = []

    def pieces(source, target, first, size, count):
        for piece in range(count):
            rows = pl.ds(first + piece * (size // count), size // count)
            copies.append(
                pltpu.make_async_copy(source.at[rows], target.at[rows], sems.at[2 + len(copies)])
            )
            copies[-1].start()

    pieces(items_in, items, 0, ROWS, 1)
    waits = []
    for batch in range(BATCHES):
        pieces(users_in, users, batch * ROWS, ROWS, 1)
        pieces(ratings_in, tiles, batch * SLOTS, SLOTS, 1)
        waits.append(len(copies))
    tiles[LISTED] = jnp.zeros((TILE, TILE), BF16)
    for copy in list_copies:
        copy.wait()
    place_slots(where, lists, counts, 0)
    halves = [None] * HALVES
    user_parts = {}

    def users_of(batch):
        if batch not in user_parts:
            user_parts[batch] = split(users[batch_rows(batch)])
        return user_parts[batch]

    def before(kind, half, batch):
        if kind == "P" and half == 0 and batch == 0:
            for copy in copies[: waits[0]]:
                copy.wait()
        if kind == "P" and batch == 0:
            halves[half] = items[half * HALF : (half + 1) * HALF]
        if kind == "P" and half == 0 and batch == 1:
            for copy in copies[waits[0] :]:
                copy.wait()

    block_steps(
        lambda batch, place: tiles[where[batch * (PLACES + 1) + place]],
        users_of,
        halves,
        residues_out,
        blocks_out,
        before,
    )
    store_coded(halves, items_out)


def first_users_kernel(
    lists_in, counts_in, ratings_in, users, residues, blocks,
    users_out, parts_out, later_out,
    tiles, lists, counts, where, sems,
):
    list_copies = fetch_lists(lists_in, counts_in, lists, counts, sems)
    tile_copies = [
        fetch_tiles(ratings_in, tiles, 1, batch, sems.at[2 + batch]) for batch in range(BATCHES)
    ]
    tiles[LISTED] = jnp.zeros((TILE, TILE), BF16)
    for batch in range(BATCHES):
        rows = batch_rows(batch)
        new = users_step(users[rows], residues, blocks, batch)
        users_out[rows] = new
        parts_out[0, rows], parts_out[1, rows] = split(new)
    for copy in list_copies:
        copy.wait()
    for copy in tile_copies:
        copy.wait()
    place_slots(where, lists, counts, 1)
    for batch in range(BATCHES):
        for place in range(PLACES):
            later_out[batch * PLACES + place] = tiles[where[batch * (PLACES + 1) + place]]


def second_block_kernel(parts, items_in, later, items_out, residues_out, blocks_out):
    halves = [decode(items_in[half, :HALF], items_in[half, HALF:]) for half in range(HALVES)]
    block_steps(
        lambda batch, place: later[batch * PLACES + place],
        lambda batch: (parts[0, batch_rows(batch)], parts[1, batch_rows(batch)]),
        halves,
        residues_out,
        blocks_out,
    )
    store_coded(halves, items_out)


def second_users_kernel(users, residues, blocks, users_out, fresh, sems):
    copies = []
    for batch in range(BATCHES):
        rows = batch_rows(batch)
        fresh[rows] = users_step(users[rows], residues, blocks, batch)
        copies.append(
            pltpu.make_async_copy(fresh.at[rows], users_out.at[rows], sems.at[batch])
        )
        copies[-1].start()
    for copy in copies:
        copy.wait()


def held(value):
    return pltpu.with_memory_space_constraint(value, pltpu.HBM)


SPEC_HBM = pl.BlockSpec(memory_space=pltpu.HBM)
SPEC_VMEM = pl.BlockSpec(memory_space=pltpu.VMEM)
CODED_SHAPE = jax.ShapeDtypeStruct((HALVES, CODED, RANK), jnp.int16)
USERS_SHAPE = jax.ShapeDtypeStruct((BATCHES * ROWS, RANK), F32)
PARTS_SHAPE = jax.ShapeDtypeStruct((2, BATCHES * ROWS, RANK), BF16)
LATER_SHAPE = jax.ShapeDtypeStruct((BATCHES * PLACES, TILE, TILE), BF16)
RESIDUES_SHAPE = jax.ShapeDtypeStruct((BATCHES, 2, ROWS, ROWS), BF16)
BLOCKS_SHAPE = jax.ShapeDtypeStruct((BATCHES, 2, ROWS, RANK), BF16)
PRODUCT_FLOPS = 2 * 3 * BATCHES * ROWS * ROWS * RANK


def call(kernel, name, outs, out_specs, in_specs, scratch, products, args):
    return pl.pallas_call(
        kernel,
        out_shape=outs,
        in_specs=in_specs,
        out_specs=out_specs,
        scratch_shapes=scratch,
        compiler_params=pltpu.CompilerParams(vmem_limit_bytes=28 * 1024 * 1024),
        cost_estimate=pl.CostEstimate(
            flops=products * PRODUCT_FLOPS, bytes_accessed=1 << 20, transcendentals=0
        ),
        name=name,
    )(*args)


def list_scratch():
    return [
        pltpu.VMEM((LISTED + 1, TILE, TILE), BF16),
        pltpu.SMEM((ENTRIES, 2, SLOTS), jnp.int32),
        pltpu.SMEM((ENTRIES,), jnp.int32),
        pltpu.SMEM((BATCHES * (PLACES + 1),), jnp.int32),
    ]


def first_block(lists, counts, users, items, ratings):
    return call(
        first_block_kernel,
        "first_block",
        (USERS_SHAPE, CODED_SHAPE, RESIDUES_SHAPE, BLOCKS_SHAPE),
        (SPEC_VMEM,) * 4,
        [SPEC_HBM] * 5,
        [pltpu.VMEM((ROWS, RANK), F32), *list_scratch(), pltpu.SemaphoreType.DMA((7,))],
        2,
        (held(lists), held(counts), held(users), held(items), held(ratings)),
    )


def first_users(lists, counts, ratings, users, residues, blocks):
    return call(
        first_users_kernel,
        "first_users",
        (USERS_SHAPE, PARTS_SHAPE, LATER_SHAPE),
        (SPEC_VMEM,) * 3,
        [SPEC_HBM] * 3 + [SPEC_VMEM] * 3,
        [*list_scratch(), pltpu.SemaphoreType.DMA((4,))],
        1,
        (held(lists), held(counts), held(ratings), users, residues, blocks),
    )


def second_block(parts, items, later):
    return call(
        second_block_kernel,
        "second_block",
        (CODED_SHAPE, RESIDUES_SHAPE, BLOCKS_SHAPE),
        (SPEC_VMEM,) * 3,
        [SPEC_VMEM] * 3,
        [],
        2,
        (parts, items, later),
    )


def second_users(users, residues, blocks):
    return call(
        second_users_kernel,
        "second_users",
        USERS_SHAPE,
        SPEC_HBM,
        [SPEC_VMEM] * 3,
        [pltpu.VMEM((BATCHES * ROWS, RANK), F32), pltpu.SemaphoreType.DMA((BATCHES,))],
        1,
        (users, residues, blocks),
    )


PIECE = 128


def unpack_kernel(coded, items_out, items, sems):
    copies = []
    for piece in range(ROWS // PIECE):
        half, first = divmod(piece * PIECE, HALF)
        rows = pl.ds(piece * PIECE, PIECE)
        items[rows] = decode(coded[half, first : first + PIECE], coded[half, HALF:])
        copies.append(pltpu.make_async_copy(items.at[rows], items_out.at[rows], sems.at[piece]))
        copies[-1].start()
    for copy in copies:
        copy.wait()


def unpack(coded):
    return pl.pallas_call(
        unpack_kernel,
        out_shape=jax.ShapeDtypeStruct((ROWS, RANK), F32),
        in_specs=[SPEC_VMEM],
        out_specs=SPEC_HBM,
        scratch_shapes=[
            pltpu.VMEM((ROWS, RANK), F32),
            pltpu.SemaphoreType.DMA((ROWS // PIECE,)),
        ],
        compiler_params=pltpu.CompilerParams(vmem_limit_bytes=8 * 1024 * 1024),
        name="unpack",
    )(coded)


def on_device(user_factors, item_factors, ratings, tile_lists, tile_counts):
    users, coded, residues, blocks = first_block(
        tile_lists, tile_counts, user_factors, item_factors, ratings
    )
    arrived = passed_along(coded, "blk", 1)
    users, parts, later = first_users(tile_lists, tile_counts, ratings, users, residues, blocks)
    coded, residues, blocks = second_block(parts, arrived, later)
    returned = passed_along(coded, "blk", -1)
    users = second_users(users, residues, blocks)
    items = unpack(returned)
    return (users, items)


def solution(mesh):
    in_specs = (
        P(("grp", "blk"), None),
        P(("grp", "blk"), None),
        P(("grp", "blk"), None, None),
        P(("grp", "blk"), None, None),
        P(("grp", "blk")),
    )
    out_specs = (P(("grp", "blk"), None), P(("grp", "blk"), None))
    return jax.shard_map(
        on_device, mesh=mesh, in_specs=in_specs, out_specs=out_specs, check_vma=False
    )
```

```python
import jax
import jax.numpy as jnp
from jax import lax
from jax.experimental import pallas as pl
from jax.experimental.pallas import tpu as pltpu
from jax.sharding import PartitionSpec as P

TILE = 128
BATCHES = 2
VISITS = 2
SLOTS = 12
SIDE = 4
PLACES = SIDE * SIDE
ROWS = SIDE * TILE
RANK = 256
HALVES = 2
HALF = ROWS // HALVES
EXTRA = 16
ENTRIES = VISITS * BATCHES
LISTED = BATCHES * SLOTS
NONE = ENTRIES * SLOTS

LEARN = 0.02
DECAY = 0.05
TOP = 32766.0
F32 = jnp.float32
BF16 = jnp.bfloat16


def passed_along(value, axis, steps):
    count = lax.axis_size(axis)
    pairs = [(source, (source + steps) % count) for source in range(count)]
    return lax.ppermute(value, axis, pairs)


def split(value):
    high = value.astype(BF16)
    low = (value - high.astype(F32)).astype(BF16)
    return high, low


def dot(left, right, dims):
    return lax.dot_general(left, right, (dims, ((), ())), preferred_element_type=F32)


def product(left, right, dims):
    (left_dim,), (right_dim,) = dims
    wide = jnp.concatenate([left[0], left[1], left[0]], axis=left_dim)
    tall = jnp.concatenate([right[0], right[0], right[1]], axis=right_dim)
    return dot(wide, tall, dims)


def encode(block):
    peak = jnp.maximum(jnp.max(jnp.abs(block), axis=0, keepdims=True), 1e-30)
    power = jnp.ceil(jnp.log2(peak))
    unit = jnp.exp2(power - 8.0)
    units = jnp.ceil(peak / unit)
    coded = jnp.round(block * (TOP / (units * unit))).astype(jnp.int32)
    return coded.astype(jnp.int16), (power.astype(jnp.int32), units.astype(jnp.int32))


def decode(coded, half, first=0, size=HALF):
    scale = coded[ROWS:].astype(jnp.int32).astype(F32)
    power, units = scale[2 * half : 2 * half + 1], scale[2 * half + 1 : 2 * half + 2]
    step = units * jnp.exp2(power - 8.0) * (1.0 / TOP)
    start = half * HALF + first
    return coded[start : start + size].astype(jnp.int32).astype(F32) * step


def batch_rows(batch):
    return pl.ds(batch * ROWS, ROWS)


def residue_parts(predicted, observed_tile, columns):
    highs, lows = [], []
    for row in range(SIDE):
        high_row, low_row = [], []
        for column in range(columns):
            observed = observed_tile(row, column).astype(F32)
            part = predicted[row * TILE : (row + 1) * TILE, column * TILE : (column + 1) * TILE]
            high, low = split(jnp.where(observed != 0, part - observed, 0.0))
            high_row.append(high)
            low_row.append(low)
        highs.append(jnp.concatenate(high_row, axis=1))
        lows.append(jnp.concatenate(low_row, axis=1))
    return jnp.concatenate(highs, axis=0), jnp.concatenate(lows, axis=0)


ORDER = "P00 P10 R00 R10 G00 G10 P01 P11 R01 R11 G01 G11"


def block_steps(observed_tile, users_of, halves, blocks_out, before=None):
    parts, predicted, residues = {}, {}, {}
    columns = SIDE // HALVES
    for item in ORDER.split():
        kind, half, batch = item[0], int(item[1]), int(item[2])
        span = pl.ds(half * HALF, HALF)
        if before is not None:
            before(kind, half, batch)
        if kind == "P":
            parts[half] = split(halves[half])
            for which in range(2):
                blocks_out[batch, which, span] = parts[half][which]
            predicted[half] = product(users_of(batch), parts[half], ((1,), (1,)))
        elif kind == "R":
            residues[half] = residue_parts(
                predicted[half],
                lambda row, column: observed_tile(batch, row * SIDE + half * columns + column),
                columns,
            )
        else:
            grad_items = product(residues[half], users_of(batch), ((0,), (0,)))
            halves[half] = halves[half] - LEARN * (grad_items + DECAY * halves[half])


def users_step(old, parts, block, observed_tile):
    predicted = product(parts, block, ((1,), (1,)))
    residues = residue_parts(
        predicted, lambda row, column: observed_tile(row * SIDE + column), SIDE
    )
    grad_users = product(residues, block, ((1,), (0,)))
    return old - LEARN * (grad_users + DECAY * old)


def store_coded(halves, items_out):
    row = lax.broadcasted_iota(jnp.int32, (EXTRA, RANK), 0)
    scales = jnp.zeros((EXTRA, RANK), jnp.int32)
    for half in range(HALVES):
        coded, scale = encode(halves[half])
        items_out[half * HALF : (half + 1) * HALF] = coded
        for which in range(2):
            scales = jnp.where(row == 2 * half + which, scale[which], scales)
    items_out[ROWS:] = scales.astype(jnp.int16)


def place_slots(where, lists, counts, visit, first, none):
    for batch in range(BATCHES):
        entry = visit * BATCHES + batch
        base = (first + batch) * (PLACES + 1)
        count = counts[entry]
        for place in range(PLACES):
            where[base + place] = none
        for slot in range(SLOTS):
            row = jnp.clip(lists[entry, 0, slot], 0, SIDE - 1)
            column = jnp.clip(lists[entry, 1, slot], 0, SIDE - 1)
            target = jnp.where(slot < count, row * SIDE + column, PLACES)
            where[base + target] = (first + batch) * SLOTS + slot


def fetch_lists(lists_in, counts_in, lists, counts, sems):
    copies = (
        pltpu.make_async_copy(lists_in, lists, sems.at[0]),
        pltpu.make_async_copy(counts_in, counts, sems.at[1]),
    )
    for copy in copies:
        copy.start()
    return copies


def fetch_tiles(ratings_in, tiles, visit, batch, sem):
    slots = pl.ds((visit * BATCHES + batch) * SLOTS, SLOTS)
    copy = pltpu.make_async_copy(ratings_in.at[slots], tiles.at[slots], sem)
    copy.start()
    return copy


def first_block_kernel(
    lists_in, counts_in, users_in, items_in, ratings_in,
    users, items_out, blocks_out,
    items, tiles, lists, counts, where, sems,
):
    list_copies = fetch_lists(lists_in, counts_in, lists, counts, sems)
    copies = []

    def pieces(source, target, first, size, count):
        for piece in range(count):
            rows = pl.ds(first + piece * (size // count), size // count)
            copies.append(
                pltpu.make_async_copy(source.at[rows], target.at[rows], sems.at[2 + len(copies)])
            )
            copies[-1].start()

    pieces(items_in, items, 0, ROWS, 1)
    waits = []
    for batch in range(BATCHES):
        pieces(users_in, users, batch * ROWS, ROWS, 1)
        pieces(ratings_in, tiles, batch * SLOTS, SLOTS, 1)
        waits.append(len(copies))
    tiles[LISTED] = jnp.zeros((TILE, TILE), BF16)
    for copy in list_copies:
        copy.wait()
    place_slots(where, lists, counts, 0, 0, LISTED)
    halves = [None] * HALVES
    user_parts = {}

    def users_of(batch):
        if batch not in user_parts:
            user_parts[batch] = split(users[batch_rows(batch)])
        return user_parts[batch]

    def before(kind, half, batch):
        if kind == "P" and half == 0 and batch == 0:
            for copy in copies[: waits[0]]:
                copy.wait()
        if kind == "P" and batch == 0:
            halves[half] = items[half * HALF : (half + 1) * HALF]
        if kind == "P" and half == 0 and batch == 1:
            for copy in copies[waits[0] :]:
                copy.wait()

    block_steps(
        lambda batch, place: tiles[where[batch * (PLACES + 1) + place]],
        users_of,
        halves,
        blocks_out,
        before,
    )
    store_coded(halves, items_out)


def first_users_kernel(
    lists_in, counts_in, ratings_in, users, blocks,
    users_out, parts_out, later_out,
    tiles, lists, counts, where, sems,
):
    list_copies = fetch_lists(lists_in, counts_in, lists, counts, sems)
    tile_copies = [
        fetch_tiles(ratings_in, tiles, visit, batch, sems.at[2 + visit * BATCHES + batch])
        for visit in range(VISITS)
        for batch in range(BATCHES)
    ]
    tiles[NONE] = jnp.zeros((TILE, TILE), BF16)
    for copy in list_copies + tuple(tile_copies):
        copy.wait()
    for visit in range(VISITS):
        place_slots(where, lists, counts, visit, visit * BATCHES, NONE)
    for batch in range(BATCHES):
        rows = batch_rows(batch)
        old = users[rows]
        new = users_step(
            old,
            split(old),
            (blocks[batch, 0], blocks[batch, 1]),
            lambda place: tiles[where[batch * (PLACES + 1) + place]],
        )
        users_out[rows] = new
        parts_out[0, rows], parts_out[1, rows] = split(new)
    for batch in range(BATCHES):
        for place in range(PLACES):
            slot = where[(BATCHES + batch) * (PLACES + 1) + place]
            later_out[batch * PLACES + place] = tiles[slot]


def second_block_kernel(parts, items_in, later, items_out, blocks_out):
    halves = [decode(items_in, half) for half in range(HALVES)]
    block_steps(
        lambda batch, place: later[batch * PLACES + place],
        lambda batch: (parts[0, batch_rows(batch)], parts[1, batch_rows(batch)]),
        halves,
        blocks_out,
    )
    store_coded(halves, items_out)


def second_users_kernel(users, parts, blocks, later, users_out, fresh, sems):
    copies = []
    for batch in range(BATCHES):
        rows = batch_rows(batch)
        fresh[rows] = users_step(
            users[rows],
            (parts[0, rows], parts[1, rows]),
            (blocks[batch, 0], blocks[batch, 1]),
            lambda place: later[batch * PLACES + place],
        )
        copies.append(
            pltpu.make_async_copy(fresh.at[rows], users_out.at[rows], sems.at[batch])
        )
        copies[-1].start()
    for copy in copies:
        copy.wait()


def held(value):
    return pltpu.with_memory_space_constraint(value, pltpu.HBM)


SPEC_HBM = pl.BlockSpec(memory_space=pltpu.HBM)
SPEC_VMEM = pl.BlockSpec(memory_space=pltpu.VMEM)
CODED_SHAPE = jax.ShapeDtypeStruct((ROWS + EXTRA, RANK), jnp.int16)
USERS_SHAPE = jax.ShapeDtypeStruct((BATCHES * ROWS, RANK), F32)
PARTS_SHAPE = jax.ShapeDtypeStruct((2, BATCHES * ROWS, RANK), BF16)
LATER_SHAPE = jax.ShapeDtypeStruct((BATCHES * PLACES, TILE, TILE), BF16)
BLOCKS_SHAPE = jax.ShapeDtypeStruct((BATCHES, 2, ROWS, RANK), BF16)
PRODUCT_FLOPS = 2 * 3 * BATCHES * ROWS * ROWS * RANK


def call(kernel, name, outs, out_specs, in_specs, scratch, products, args):
    return pl.pallas_call(
        kernel,
        out_shape=outs,
        in_specs=in_specs,
        out_specs=out_specs,
        scratch_shapes=scratch,
        compiler_params=pltpu.CompilerParams(vmem_limit_bytes=28 * 1024 * 1024),
        cost_estimate=pl.CostEstimate(
            flops=products * PRODUCT_FLOPS, bytes_accessed=1 << 20, transcendentals=0
        ),
        name=name,
    )(*args)


def list_scratch(visits):
    return [
        pltpu.VMEM((visits * LISTED + 1, TILE, TILE), BF16),
        pltpu.SMEM((ENTRIES, 2, SLOTS), jnp.int32),
        pltpu.SMEM((ENTRIES,), jnp.int32),
        pltpu.SMEM((visits * BATCHES * (PLACES + 1),), jnp.int32),
    ]


def first_block(lists, counts, users, items, ratings):
    return call(
        first_block_kernel,
        "first_block",
        (USERS_SHAPE, CODED_SHAPE, BLOCKS_SHAPE),
        (SPEC_VMEM,) * 3,
        [SPEC_HBM] * 5,
        [pltpu.VMEM((ROWS, RANK), F32), *list_scratch(1), pltpu.SemaphoreType.DMA((7,))],
        2,
        (held(lists), held(counts), held(users), held(items), held(ratings)),
    )


def first_users(lists, counts, ratings, users, blocks):
    return call(
        first_users_kernel,
        "first_users",
        (USERS_SHAPE, PARTS_SHAPE, LATER_SHAPE),
        (SPEC_VMEM,) * 3,
        [SPEC_HBM] * 3 + [SPEC_VMEM] * 2,
        [*list_scratch(VISITS), pltpu.SemaphoreType.DMA((2 + ENTRIES,))],
        2,
        (held(lists), held(counts), held(ratings), users, blocks),
    )


def second_block(parts, items, later):
    return call(
        second_block_kernel,
        "second_block",
        (CODED_SHAPE, BLOCKS_SHAPE),
        (SPEC_VMEM,) * 2,
        [SPEC_VMEM] * 3,
        [],
        2,
        (parts, items, later),
    )


def second_users(users, parts, blocks, later):
    return call(
        second_users_kernel,
        "second_users",
        USERS_SHAPE,
        SPEC_HBM,
        [SPEC_VMEM] * 4,
        [pltpu.VMEM((BATCHES * ROWS, RANK), F32), pltpu.SemaphoreType.DMA((BATCHES,))],
        2,
        (users, parts, blocks, later),
    )


PIECE = 128


def unpack_kernel(coded, items_out, items, sems):
    copies = []
    for piece in range(ROWS // PIECE):
        half, first = divmod(piece * PIECE, HALF)
        rows = pl.ds(piece * PIECE, PIECE)
        items[rows] = decode(coded, half, first, PIECE)
        copies.append(pltpu.make_async_copy(items.at[rows], items_out.at[rows], sems.at[piece]))
        copies[-1].start()
    for copy in copies:
        copy.wait()


def unpack(coded):
    return pl.pallas_call(
        unpack_kernel,
        out_shape=jax.ShapeDtypeStruct((ROWS, RANK), F32),
        in_specs=[SPEC_VMEM],
        out_specs=SPEC_HBM,
        scratch_shapes=[
            pltpu.VMEM((ROWS, RANK), F32),
            pltpu.SemaphoreType.DMA((ROWS // PIECE,)),
        ],
        compiler_params=pltpu.CompilerParams(vmem_limit_bytes=8 * 1024 * 1024),
        name="unpack",
    )(coded)


def on_device(user_factors, item_factors, ratings, tile_lists, tile_counts):
    users, coded, blocks = first_block(
        tile_lists, tile_counts, user_factors, item_factors, ratings
    )
    arrived = passed_along(coded, "blk", 1)
    users, parts, later = first_users(tile_lists, tile_counts, ratings, users, blocks)
    coded, blocks = second_block(parts, arrived, later)
    returned = passed_along(coded, "blk", -1)
    users = second_users(users, parts, blocks, later)
    items = unpack(returned)
    return (users, items)


def solution(mesh):
    in_specs = (
        P(("grp", "blk"), None),
        P(("grp", "blk"), None),
        P(("grp", "blk"), None, None),
        P(("grp", "blk"), None, None),
        P(("grp", "blk")),
    )
    out_specs = (P(("grp", "blk"), None), P(("grp", "blk"), None))
    return jax.shard_map(
        on_device, mesh=mesh, in_specs=in_specs, out_specs=out_specs, check_vma=False
    )
```

```python
import jax
import jax.numpy as jnp
from jax import lax
from jax.experimental import pallas as pl
from jax.experimental.pallas import tpu as pltpu
from jax.sharding import PartitionSpec as P

TILE = 128
BATCHES = 2
VISITS = 2
SLOTS = 12
SIDE = 4
PLACES = SIDE * SIDE
ROWS = SIDE * TILE
RANK = 256
HALVES = 2
HALF = ROWS // HALVES
EXTRA = 16
ENTRIES = VISITS * BATCHES
LISTED = BATCHES * SLOTS
NONE = ENTRIES * SLOTS

LEARN = 0.02
DECAY = 0.05
TOP = 32766.0
F32 = jnp.float32
BF16 = jnp.bfloat16


def passed_along(value, axis, steps):
    count = lax.axis_size(axis)
    pairs = [(source, (source + steps) % count) for source in range(count)]
    return lax.ppermute(value, axis, pairs)


def split(value):
    high = value.astype(BF16)
    low = (value - high.astype(F32)).astype(BF16)
    return high, low


def dot(left, right, dims):
    return lax.dot_general(left, right, (dims, ((), ())), preferred_element_type=F32)


def product(left, right, dims):
    (left_dim,), (right_dim,) = dims
    wide = jnp.concatenate([left[0], left[1], left[0]], axis=left_dim)
    tall = jnp.concatenate([right[0], right[0], right[1]], axis=right_dim)
    return dot(wide, tall, dims)


def encode(block):
    peak = jnp.maximum(jnp.max(jnp.abs(block), axis=0, keepdims=True), 1e-30)
    power = jnp.ceil(jnp.log2(peak))
    unit = jnp.exp2(power - 8.0)
    units = jnp.ceil(peak / unit)
    coded = jnp.round(block * (TOP / (units * unit))).astype(jnp.int32)
    return coded.astype(jnp.int16), (power.astype(jnp.int32), units.astype(jnp.int32))


def decode(coded, half, first=0, size=HALF):
    scale = coded[ROWS:].astype(jnp.int32).astype(F32)
    power, units = scale[2 * half : 2 * half + 1], scale[2 * half + 1 : 2 * half + 2]
    step = units * jnp.exp2(power - 8.0) * (1.0 / TOP)
    start = half * HALF + first
    return coded[start : start + size].astype(jnp.int32).astype(F32) * step


def batch_rows(batch):
    return pl.ds(batch * ROWS, ROWS)


def residue_parts(predicted, observed_tile, columns):
    highs, lows = [], []
    for row in range(SIDE):
        high_row, low_row = [], []
        for column in range(columns):
            observed = observed_tile(row, column).astype(F32)
            part = predicted[row * TILE : (row + 1) * TILE, column * TILE : (column + 1) * TILE]
            high, low = split(jnp.where(observed != 0, part - observed, 0.0))
            high_row.append(high)
            low_row.append(low)
        highs.append(jnp.concatenate(high_row, axis=1))
        lows.append(jnp.concatenate(low_row, axis=1))
    return jnp.concatenate(highs, axis=0), jnp.concatenate(lows, axis=0)


ORDER = tuple(
    (kind, half, batch) for batch in range(BATCHES) for kind in "PRG" for half in range(HALVES)
)


def block_steps(observed_tile, users_of, halves, blocks_out, before=None):
    parts, predicted, residues = {}, {}, {}
    columns = SIDE // HALVES
    for kind, half, batch in ORDER:
        span = pl.ds(half * HALF, HALF)
        if before is not None:
            before(kind, half, batch)
        if kind == "P":
            parts[half] = split(halves[half])
            for which in range(2):
                blocks_out[batch, which, span] = parts[half][which]
            predicted[half] = product(users_of(batch), parts[half], ((1,), (1,)))
        elif kind == "R":
            residues[half] = residue_parts(
                predicted[half],
                lambda row, column: observed_tile(batch, row * SIDE + half * columns + column),
                columns,
            )
        else:
            grad_items = product(residues[half], users_of(batch), ((0,), (0,)))
            halves[half] = halves[half] - LEARN * (grad_items + DECAY * halves[half])


def users_step(old, parts, block, observed_tile):
    predicted = product(parts, block, ((1,), (1,)))
    residues = residue_parts(
        predicted, lambda row, column: observed_tile(row * SIDE + column), SIDE
    )
    grad_users = product(residues, block, ((1,), (0,)))
    return old - LEARN * (grad_users + DECAY * old)


def store_coded(halves, items_out):
    row = lax.broadcasted_iota(jnp.int32, (EXTRA, RANK), 0)
    scales = jnp.zeros((EXTRA, RANK), jnp.int32)
    for half in range(HALVES):
        coded, scale = encode(halves[half])
        items_out[half * HALF : (half + 1) * HALF] = coded
        for which in range(2):
            scales = jnp.where(row == 2 * half + which, scale[which], scales)
    items_out[ROWS:] = scales.astype(jnp.int16)


def place_slots(where, lists, counts, visit, first, none):
    for batch in range(BATCHES):
        entry = visit * BATCHES + batch
        base = (first + batch) * (PLACES + 1)
        count = counts[entry]
        for place in range(PLACES):
            where[base + place] = none
        for slot in range(SLOTS):
            row = jnp.clip(lists[entry, 0, slot], 0, SIDE - 1)
            column = jnp.clip(lists[entry, 1, slot], 0, SIDE - 1)
            target = jnp.where(slot < count, row * SIDE + column, PLACES)
            where[base + target] = (first + batch) * SLOTS + slot


def fetch_lists(lists_in, counts_in, lists, counts, sems):
    copies = (
        pltpu.make_async_copy(lists_in, lists, sems.at[0]),
        pltpu.make_async_copy(counts_in, counts, sems.at[1]),
    )
    for copy in copies:
        copy.start()
    return copies


def fetch_tiles(ratings_in, tiles, visit, batch, sem):
    slots = pl.ds((visit * BATCHES + batch) * SLOTS, SLOTS)
    copy = pltpu.make_async_copy(ratings_in.at[slots], tiles.at[slots], sem)
    copy.start()
    return copy


def first_block_kernel(
    lists_in, counts_in, users_in, items_in, ratings_in,
    users, items_out, blocks_out,
    items, tiles, lists, counts, where, sems,
):
    list_copies = fetch_lists(lists_in, counts_in, lists, counts, sems)
    copies = []

    def pieces(source, target, first, size, count):
        for piece in range(count):
            rows = pl.ds(first + piece * (size // count), size // count)
            copies.append(
                pltpu.make_async_copy(source.at[rows], target.at[rows], sems.at[2 + len(copies)])
            )
            copies[-1].start()

    pieces(items_in, items, 0, ROWS, 1)
    waits = []
    for batch in range(BATCHES):
        pieces(users_in, users, batch * ROWS, ROWS, 1)
        pieces(ratings_in, tiles, batch * SLOTS, SLOTS, 1)
        waits.append(len(copies))
    tiles[LISTED] = jnp.zeros((TILE, TILE), BF16)
    for copy in list_copies:
        copy.wait()
    place_slots(where, lists, counts, 0, 0, LISTED)
    halves = [None] * HALVES
    user_parts = {}

    def users_of(batch):
        if batch not in user_parts:
            user_parts[batch] = split(users[batch_rows(batch)])
        return user_parts[batch]

    def before(kind, half, batch):
        if kind == "P" and half == 0 and batch == 0:
            for copy in copies[: waits[0]]:
                copy.wait()
        if kind == "P" and batch == 0:
            halves[half] = items[half * HALF : (half + 1) * HALF]
        if kind == "P" and half == 0 and batch == 1:
            for copy in copies[waits[0] :]:
                copy.wait()

    block_steps(
        lambda batch, place: tiles[where[batch * (PLACES + 1) + place]],
        users_of,
        halves,
        blocks_out,
        before,
    )
    store_coded(halves, items_out)


def first_users_kernel(
    lists_in, counts_in, ratings_in, users, blocks,
    users_out, parts_out, later_out,
    tiles, lists, counts, where, sems,
):
    list_copies = fetch_lists(lists_in, counts_in, lists, counts, sems)
    tile_copies = [
        fetch_tiles(ratings_in, tiles, visit, batch, sems.at[2 + visit * BATCHES + batch])
        for visit in range(VISITS)
        for batch in range(BATCHES)
    ]
    tiles[NONE] = jnp.zeros((TILE, TILE), BF16)
    for copy in list_copies + tuple(tile_copies):
        copy.wait()
    for visit in range(VISITS):
        place_slots(where, lists, counts, visit, visit * BATCHES, NONE)
    for batch in range(BATCHES):
        rows = batch_rows(batch)
        old = users[rows]
        new = users_step(
            old,
            split(old),
            (blocks[batch, 0], blocks[batch, 1]),
            lambda place: tiles[where[batch * (PLACES + 1) + place]],
        )
        users_out[rows] = new
        parts_out[0, rows], parts_out[1, rows] = split(new)
    for batch in range(BATCHES):
        for place in range(PLACES):
            slot = where[(BATCHES + batch) * (PLACES + 1) + place]
            later_out[batch * PLACES + place] = tiles[slot]


def second_block_kernel(parts, items_in, later, items_out, blocks_out):
    halves = [decode(items_in, half) for half in range(HALVES)]
    block_steps(
        lambda batch, place: later[batch * PLACES + place],
        lambda batch: (parts[0, batch_rows(batch)], parts[1, batch_rows(batch)]),
        halves,
        blocks_out,
    )
    store_coded(halves, items_out)


def second_users_kernel(users, parts, blocks, later, users_out, fresh, sems):
    copies = []
    for batch in range(BATCHES):
        rows = batch_rows(batch)
        fresh[rows] = users_step(
            users[rows],
            (parts[0, rows], parts[1, rows]),
            (blocks[batch, 0], blocks[batch, 1]),
            lambda place: later[batch * PLACES + place],
        )
        copies.append(
            pltpu.make_async_copy(fresh.at[rows], users_out.at[rows], sems.at[batch])
        )
        copies[-1].start()
    for copy in copies:
        copy.wait()


def held(value):
    return pltpu.with_memory_space_constraint(value, pltpu.HBM)


SPEC_HBM = pl.BlockSpec(memory_space=pltpu.HBM)
SPEC_VMEM = pl.BlockSpec(memory_space=pltpu.VMEM)
CODED_SHAPE = jax.ShapeDtypeStruct((ROWS + EXTRA, RANK), jnp.int16)
USERS_SHAPE = jax.ShapeDtypeStruct((BATCHES * ROWS, RANK), F32)
PARTS_SHAPE = jax.ShapeDtypeStruct((2, BATCHES * ROWS, RANK), BF16)
LATER_SHAPE = jax.ShapeDtypeStruct((BATCHES * PLACES, TILE, TILE), BF16)
BLOCKS_SHAPE = jax.ShapeDtypeStruct((BATCHES, 2, ROWS, RANK), BF16)
PRODUCT_FLOPS = 2 * 3 * BATCHES * ROWS * ROWS * RANK


def call(kernel, name, outs, out_specs, in_specs, scratch, products, args):
    return pl.pallas_call(
        kernel,
        out_shape=outs,
        in_specs=in_specs,
        out_specs=out_specs,
        scratch_shapes=scratch,
        compiler_params=pltpu.CompilerParams(vmem_limit_bytes=28 * 1024 * 1024),
        cost_estimate=pl.CostEstimate(
            flops=products * PRODUCT_FLOPS, bytes_accessed=1 << 20, transcendentals=0
        ),
        name=name,
    )(*args)


def list_scratch(visits):
    return [
        pltpu.VMEM((visits * LISTED + 1, TILE, TILE), BF16),
        pltpu.SMEM((ENTRIES, 2, SLOTS), jnp.int32),
        pltpu.SMEM((ENTRIES,), jnp.int32),
        pltpu.SMEM((visits * BATCHES * (PLACES + 1),), jnp.int32),
    ]


def first_block(lists, counts, users, items, ratings):
    return call(
        first_block_kernel,
        "first_block",
        (USERS_SHAPE, CODED_SHAPE, BLOCKS_SHAPE),
        (SPEC_VMEM,) * 3,
        [SPEC_HBM] * 5,
        [pltpu.VMEM((ROWS, RANK), F32), *list_scratch(1), pltpu.SemaphoreType.DMA((7,))],
        2,
        (held(lists), held(counts), held(users), held(items), held(ratings)),
    )


def first_users(lists, counts, ratings, users, blocks):
    return call(
        first_users_kernel,
        "first_users",
        (USERS_SHAPE, PARTS_SHAPE, LATER_SHAPE),
        (SPEC_VMEM,) * 3,
        [SPEC_HBM] * 3 + [SPEC_VMEM] * 2,
        [*list_scratch(VISITS), pltpu.SemaphoreType.DMA((2 + ENTRIES,))],
        2,
        (held(lists), held(counts), held(ratings), users, blocks),
    )


def second_block(parts, items, later):
    return call(
        second_block_kernel,
        "second_block",
        (CODED_SHAPE, BLOCKS_SHAPE),
        (SPEC_VMEM,) * 2,
        [SPEC_VMEM] * 3,
        [],
        2,
        (parts, items, later),
    )


def second_users(users, parts, blocks, later):
    return call(
        second_users_kernel,
        "second_users",
        USERS_SHAPE,
        SPEC_HBM,
        [SPEC_VMEM] * 4,
        [pltpu.VMEM((BATCHES * ROWS, RANK), F32), pltpu.SemaphoreType.DMA((BATCHES,))],
        2,
        (users, parts, blocks, later),
    )


PIECE = 128


def unpack_kernel(coded, items_out, items, sems):
    copies = []
    for piece in range(ROWS // PIECE):
        half, first = divmod(piece * PIECE, HALF)
        rows = pl.ds(piece * PIECE, PIECE)
        items[rows] = decode(coded, half, first, PIECE)
        copies.append(pltpu.make_async_copy(items.at[rows], items_out.at[rows], sems.at[piece]))
        copies[-1].start()
    for copy in copies:
        copy.wait()


def unpack(coded):
    return pl.pallas_call(
        unpack_kernel,
        out_shape=jax.ShapeDtypeStruct((ROWS, RANK), F32),
        in_specs=[SPEC_VMEM],
        out_specs=SPEC_HBM,
        scratch_shapes=[
            pltpu.VMEM((ROWS, RANK), F32),
            pltpu.SemaphoreType.DMA((ROWS // PIECE,)),
        ],
        compiler_params=pltpu.CompilerParams(vmem_limit_bytes=8 * 1024 * 1024),
        name="unpack",
    )(coded)


def on_device(user_factors, item_factors, ratings, tile_lists, tile_counts):
    users, coded, blocks = first_block(
        tile_lists, tile_counts, user_factors, item_factors, ratings
    )
    arrived = passed_along(coded, "blk", 1)
    users, parts, later = first_users(tile_lists, tile_counts, ratings, users, blocks)
    coded, blocks = second_block(parts, arrived, later)
    returned = passed_along(coded, "blk", -1)
    users = second_users(users, parts, blocks, later)
    items = unpack(returned)
    return (users, items)


def solution(mesh):
    in_specs = (
        P(("grp", "blk"), None),
        P(("grp", "blk"), None),
        P(("grp", "blk"), None, None),
        P(("grp", "blk"), None, None),
        P(("grp", "blk")),
    )
    out_specs = (P(("grp", "blk"), None), P(("grp", "blk"), None))
    return jax.shard_map(
        on_device, mesh=mesh, in_specs=in_specs, out_specs=out_specs, check_vma=False
    )
```

```python
import jax
import jax.numpy as jnp
from jax import lax
from jax.experimental import pallas as pl
from jax.experimental.pallas import tpu as pltpu
from jax.sharding import PartitionSpec as P

TILE = 128
BATCHES = 2
VISITS = 2
SLOTS = 12
SIDE = 4
PLACES = SIDE * SIDE
ROWS = SIDE * TILE
RANK = 256
HALVES = 2
HALF = ROWS // HALVES
PIECES = 2
EXTRA = 16
ENTRIES = VISITS * BATCHES
LISTED = BATCHES * SLOTS
NONE = ENTRIES * SLOTS

LEARN = 0.02
DECAY = 0.05
TOP = 32766.0
F32 = jnp.float32
BF16 = jnp.bfloat16


def passed_along(value, axis, steps):
    count = lax.axis_size(axis)
    pairs = [(source, (source + steps) % count) for source in range(count)]
    return lax.ppermute(value, axis, pairs)


def split(value):
    high = value.astype(BF16)
    low = (value - high.astype(F32)).astype(BF16)
    return high, low


def dot(left, right, dims):
    return lax.dot_general(left, right, (dims, ((), ())), preferred_element_type=F32)


def product(left, right, dims):
    (left_dim,), (right_dim,) = dims
    wide = jnp.concatenate([left[0], left[1], left[0]], axis=left_dim)
    tall = jnp.concatenate([right[0], right[0], right[1]], axis=right_dim)
    return dot(wide, tall, dims)


def encode(block):
    peak = jnp.maximum(jnp.max(jnp.abs(block), axis=0, keepdims=True), 1e-30)
    power = jnp.ceil(jnp.log2(peak))
    unit = jnp.exp2(power - 8.0)
    units = jnp.ceil(peak / unit)
    coded = jnp.round(block * (TOP / (units * unit))).astype(jnp.int32)
    return coded.astype(jnp.int16), (power.astype(jnp.int32), units.astype(jnp.int32))


def decode(coded, half, first=0, size=HALF):
    scale = coded[ROWS:].astype(jnp.int32).astype(F32)
    power, units = scale[2 * half : 2 * half + 1], scale[2 * half + 1 : 2 * half + 2]
    step = units * jnp.exp2(power - 8.0) * (1.0 / TOP)
    start = half * HALF + first
    return coded[start : start + size].astype(jnp.int32).astype(F32) * step


def batch_rows(batch):
    return pl.ds(batch * ROWS, ROWS)


def residue_parts(predicted, observed_tile, columns):
    highs, lows = [], []
    for row in range(predicted.shape[0] // TILE):
        high_row, low_row = [], []
        for column in range(columns):
            observed = observed_tile(row, column).astype(F32)
            part = predicted[row * TILE : (row + 1) * TILE, column * TILE : (column + 1) * TILE]
            high, low = split(jnp.where(observed != 0, part - observed, 0.0))
            high_row.append(high)
            low_row.append(low)
        highs.append(jnp.concatenate(high_row, axis=1))
        lows.append(jnp.concatenate(low_row, axis=1))
    return jnp.concatenate(highs, axis=0), jnp.concatenate(lows, axis=0)


def user_piece(parts, piece):
    size = ROWS // PIECES
    return tuple(which[piece * size : (piece + 1) * size] for which in parts)


ORDER = tuple(
    (kind, half, batch) for batch in range(BATCHES) for kind in "PRG" for half in range(HALVES)
)


def block_steps(observed_tile, users_of, halves, blocks_out, before=None):
    parts, predicted, residues = {}, {}, {}
    columns = SIDE // HALVES
    for kind, half, batch in ORDER:
        span = pl.ds(half * HALF, HALF)
        if before is not None:
            before(kind, half, batch)
        if kind == "P":
            parts[half] = split(halves[half])
            for which in range(2):
                blocks_out[batch, which, span] = parts[half][which]
            predicted[half] = [
                product(user_piece(users_of(batch), piece), parts[half], ((1,), (1,)))
                for piece in range(PIECES)
            ]
        elif kind == "R":
            residues[half] = [
                residue_parts(
                    predicted[half][piece],
                    lambda row, column: observed_tile(
                        batch, (row + piece * (SIDE // PIECES)) * SIDE + half * columns + column
                    ),
                    columns,
                )
                for piece in range(PIECES)
            ]
        else:
            whole = tuple(jnp.concatenate(which, axis=0) for which in zip(*residues[half]))
            grad_items = product(whole, users_of(batch), ((0,), (0,)))
            halves[half] = halves[half] - LEARN * (grad_items + DECAY * halves[half])


def users_step(old, parts, block, observed_tile):
    predicted = product(parts, block, ((1,), (1,)))
    residues = residue_parts(
        predicted, lambda row, column: observed_tile(row * SIDE + column), SIDE
    )
    grad_users = product(residues, block, ((1,), (0,)))
    return old - LEARN * (grad_users + DECAY * old)


def store_coded(halves, items_out):
    row = lax.broadcasted_iota(jnp.int32, (EXTRA, RANK), 0)
    scales = jnp.zeros((EXTRA, RANK), jnp.int32)
    for half in range(HALVES):
        coded, scale = encode(halves[half])
        items_out[half * HALF : (half + 1) * HALF] = coded
        for which in range(2):
            scales = jnp.where(row == 2 * half + which, scale[which], scales)
    items_out[ROWS:] = scales.astype(jnp.int16)


def place_slots(where, lists, counts, visit, first, none):
    for batch in range(BATCHES):
        entry = visit * BATCHES + batch
        base = (first + batch) * (PLACES + 1)
        count = counts[entry]
        for place in range(PLACES):
            where[base + place] = none
        for slot in range(SLOTS):
            row = jnp.clip(lists[entry, 0, slot], 0, SIDE - 1)
            column = jnp.clip(lists[entry, 1, slot], 0, SIDE - 1)
            target = jnp.where(slot < count, row * SIDE + column, PLACES)
            where[base + target] = (first + batch) * SLOTS + slot


def fetch_lists(lists_in, counts_in, lists, counts, sems):
    copies = (
        pltpu.make_async_copy(lists_in, lists, sems.at[0]),
        pltpu.make_async_copy(counts_in, counts, sems.at[1]),
    )
    for copy in copies:
        copy.start()
    return copies


def fetch_tiles(ratings_in, tiles, visit, batch, sem):
    slots = pl.ds((visit * BATCHES + batch) * SLOTS, SLOTS)
    copy = pltpu.make_async_copy(ratings_in.at[slots], tiles.at[slots], sem)
    copy.start()
    return copy


def first_block_kernel(
    lists_in, counts_in, users_in, items_in, ratings_in,
    users, items_out, blocks_out,
    items, tiles, lists, counts, where, sems,
):
    list_copies = fetch_lists(lists_in, counts_in, lists, counts, sems)
    copies = []

    def pieces(source, target, first, size, count):
        for piece in range(count):
            rows = pl.ds(first + piece * (size // count), size // count)
            copies.append(
                pltpu.make_async_copy(source.at[rows], target.at[rows], sems.at[2 + len(copies)])
            )
            copies[-1].start()

    pieces(items_in, items, 0, ROWS, 1)
    waits = []
    for batch in range(BATCHES):
        pieces(users_in, users, batch * ROWS, ROWS, 1)
        pieces(ratings_in, tiles, batch * SLOTS, SLOTS, 1)
        waits.append(len(copies))
    tiles[LISTED] = jnp.zeros((TILE, TILE), BF16)
    for copy in list_copies:
        copy.wait()
    place_slots(where, lists, counts, 0, 0, LISTED)
    halves = [None] * HALVES
    user_parts = {}

    def users_of(batch):
        if batch not in user_parts:
            user_parts[batch] = split(users[batch_rows(batch)])
        return user_parts[batch]

    def before(kind, half, batch):
        if kind == "P" and half == 0 and batch == 0:
            for copy in copies[: waits[0] - 1]:
                copy.wait()
        if kind == "P" and batch == 0:
            halves[half] = items[half * HALF : (half + 1) * HALF]
        if kind == "R" and half == 0 and batch == 0:
            copies[waits[0] - 1].wait()
        if kind == "P" and half == 0 and batch == 1:
            for copy in copies[waits[0] :]:
                copy.wait()

    block_steps(
        lambda batch, place: tiles[where[batch * (PLACES + 1) + place]],
        users_of,
        halves,
        blocks_out,
        before,
    )
    store_coded(halves, items_out)


def first_users_kernel(
    lists_in, counts_in, ratings_in, users, blocks,
    users_out, parts_out, later_out,
    tiles, lists, counts, where, sems,
):
    list_copies = fetch_lists(lists_in, counts_in, lists, counts, sems)
    tile_copies = [
        fetch_tiles(ratings_in, tiles, visit, batch, sems.at[2 + visit * BATCHES + batch])
        for visit in range(VISITS)
        for batch in range(BATCHES)
    ]
    tiles[NONE] = jnp.zeros((TILE, TILE), BF16)
    for copy in list_copies + tuple(tile_copies):
        copy.wait()
    for visit in range(VISITS):
        place_slots(where, lists, counts, visit, visit * BATCHES, NONE)
    for batch in range(BATCHES):
        rows = batch_rows(batch)
        old = users[rows]
        new = users_step(
            old,
            split(old),
            (blocks[batch, 0], blocks[batch, 1]),
            lambda place: tiles[where[batch * (PLACES + 1) + place]],
        )
        users_out[rows] = new
        parts_out[0, rows], parts_out[1, rows] = split(new)
    for batch in range(BATCHES):
        for place in range(PLACES):
            slot = where[(BATCHES + batch) * (PLACES + 1) + place]
            later_out[batch * PLACES + place] = tiles[slot]


def second_block_kernel(parts, items_in, later, items_out, blocks_out):
    halves = [decode(items_in, half) for half in range(HALVES)]
    block_steps(
        lambda batch, place: later[batch * PLACES + place],
        lambda batch: (parts[0, batch_rows(batch)], parts[1, batch_rows(batch)]),
        halves,
        blocks_out,
    )
    store_coded(halves, items_out)


def second_users_kernel(users, parts, blocks, later, users_out, fresh, sems):
    copies = []
    for batch in range(BATCHES):
        rows = batch_rows(batch)
        fresh[rows] = users_step(
            users[rows],
            (parts[0, rows], parts[1, rows]),
            (blocks[batch, 0], blocks[batch, 1]),
            lambda place: later[batch * PLACES + place],
        )
        copies.append(
            pltpu.make_async_copy(fresh.at[rows], users_out.at[rows], sems.at[batch])
        )
        copies[-1].start()
    for copy in copies:
        copy.wait()


def held(value):
    return pltpu.with_memory_space_constraint(value, pltpu.HBM)


SPEC_HBM = pl.BlockSpec(memory_space=pltpu.HBM)
SPEC_VMEM = pl.BlockSpec(memory_space=pltpu.VMEM)
CODED_SHAPE = jax.ShapeDtypeStruct((ROWS + EXTRA, RANK), jnp.int16)
USERS_SHAPE = jax.ShapeDtypeStruct((BATCHES * ROWS, RANK), F32)
PARTS_SHAPE = jax.ShapeDtypeStruct((2, BATCHES * ROWS, RANK), BF16)
LATER_SHAPE = jax.ShapeDtypeStruct((BATCHES * PLACES, TILE, TILE), BF16)
BLOCKS_SHAPE = jax.ShapeDtypeStruct((BATCHES, 2, ROWS, RANK), BF16)
PRODUCT_FLOPS = 2 * 3 * BATCHES * ROWS * ROWS * RANK


def call(kernel, name, outs, out_specs, in_specs, scratch, products, args):
    return pl.pallas_call(
        kernel,
        out_shape=outs,
        in_specs=in_specs,
        out_specs=out_specs,
        scratch_shapes=scratch,
        compiler_params=pltpu.CompilerParams(vmem_limit_bytes=28 * 1024 * 1024),
        cost_estimate=pl.CostEstimate(
            flops=products * PRODUCT_FLOPS, bytes_accessed=1 << 20, transcendentals=0
        ),
        name=name,
    )(*args)


def list_scratch(visits):
    return [
        pltpu.VMEM((visits * LISTED + 1, TILE, TILE), BF16),
        pltpu.SMEM((ENTRIES, 2, SLOTS), jnp.int32),
        pltpu.SMEM((ENTRIES,), jnp.int32),
        pltpu.SMEM((visits * BATCHES * (PLACES + 1),), jnp.int32),
    ]


def first_block(lists, counts, users, items, ratings):
    return call(
        first_block_kernel,
        "first_block",
        (USERS_SHAPE, CODED_SHAPE, BLOCKS_SHAPE),
        (SPEC_VMEM,) * 3,
        [SPEC_HBM] * 5,
        [pltpu.VMEM((ROWS, RANK), F32), *list_scratch(1), pltpu.SemaphoreType.DMA((7,))],
        2,
        (held(lists), held(counts), held(users), held(items), held(ratings)),
    )


def first_users(lists, counts, ratings, users, blocks):
    return call(
        first_users_kernel,
        "first_users",
        (USERS_SHAPE, PARTS_SHAPE, LATER_SHAPE),
        (SPEC_VMEM,) * 3,
        [SPEC_HBM] * 3 + [SPEC_VMEM] * 2,
        [*list_scratch(VISITS), pltpu.SemaphoreType.DMA((2 + ENTRIES,))],
        2,
        (held(lists), held(counts), held(ratings), users, blocks),
    )


def second_block(parts, items, later):
    return call(
        second_block_kernel,
        "second_block",
        (CODED_SHAPE, BLOCKS_SHAPE),
        (SPEC_VMEM,) * 2,
        [SPEC_VMEM] * 3,
        [],
        2,
        (parts, items, later),
    )


def second_users(users, parts, blocks, later):
    return call(
        second_users_kernel,
        "second_users",
        USERS_SHAPE,
        SPEC_HBM,
        [SPEC_VMEM] * 4,
        [pltpu.VMEM((BATCHES * ROWS, RANK), F32), pltpu.SemaphoreType.DMA((BATCHES,))],
        2,
        (users, parts, blocks, later),
    )


PIECE = 128


def unpack_kernel(coded, items_out, items, sems):
    copies = []
    for piece in range(ROWS // PIECE):
        half, first = divmod(piece * PIECE, HALF)
        rows = pl.ds(piece * PIECE, PIECE)
        items[rows] = decode(coded, half, first, PIECE)
        copies.append(pltpu.make_async_copy(items.at[rows], items_out.at[rows], sems.at[piece]))
        copies[-1].start()
    for copy in copies:
        copy.wait()


def unpack(coded):
    return pl.pallas_call(
        unpack_kernel,
        out_shape=jax.ShapeDtypeStruct((ROWS, RANK), F32),
        in_specs=[SPEC_VMEM],
        out_specs=SPEC_HBM,
        scratch_shapes=[
            pltpu.VMEM((ROWS, RANK), F32),
            pltpu.SemaphoreType.DMA((ROWS // PIECE,)),
        ],
        compiler_params=pltpu.CompilerParams(vmem_limit_bytes=8 * 1024 * 1024),
        name="unpack",
    )(coded)


def on_device(user_factors, item_factors, ratings, tile_lists, tile_counts):
    users, coded, blocks = first_block(
        tile_lists, tile_counts, user_factors, item_factors, ratings
    )
    arrived = passed_along(coded, "blk", 1)
    users, parts, later = first_users(tile_lists, tile_counts, ratings, users, blocks)
    coded, blocks = second_block(parts, arrived, later)
    returned = passed_along(coded, "blk", -1)
    users = second_users(users, parts, blocks, later)
    items = unpack(returned)
    return (users, items)


def solution(mesh):
    in_specs = (
        P(("grp", "blk"), None),
        P(("grp", "blk"), None),
        P(("grp", "blk"), None, None),
        P(("grp", "blk"), None, None),
        P(("grp", "blk")),
    )
    out_specs = (P(("grp", "blk"), None), P(("grp", "blk"), None))
    return jax.shard_map(
        on_device, mesh=mesh, in_specs=in_specs, out_specs=out_specs, check_vma=False
    )
```

```python
import jax
import jax.numpy as jnp
from jax import lax
from jax.experimental import pallas as pl
from jax.experimental.pallas import tpu as pltpu
from jax.sharding import PartitionSpec as P

TILE = 128
BATCHES = 2
VISITS = 2
SLOTS = 12
SIDE = 4
PLACES = SIDE * SIDE
ROWS = SIDE * TILE
RANK = 256
HALVES = 2
HALF = ROWS // HALVES
PIECES = 2
EXTRA = 16
ENTRIES = VISITS * BATCHES
LISTED = BATCHES * SLOTS
NONE = ENTRIES * SLOTS

LEARN = 0.02
DECAY = 0.05
TOP = 32766.0
F32 = jnp.float32
BF16 = jnp.bfloat16


def passed_along(value, axis, steps):
    count = lax.axis_size(axis)
    pairs = [(source, (source + steps) % count) for source in range(count)]
    return lax.ppermute(value, axis, pairs)


def split(value):
    high = value.astype(BF16)
    low = (value - high.astype(F32)).astype(BF16)
    return high, low


def dot(left, right, dims):
    return lax.dot_general(left, right, (dims, ((), ())), preferred_element_type=F32)


def product(left, right, dims):
    (left_dim,), (right_dim,) = dims
    wide = jnp.concatenate([left[0], left[1], left[0]], axis=left_dim)
    tall = jnp.concatenate([right[0], right[0], right[1]], axis=right_dim)
    return dot(wide, tall, dims)


def encode(block):
    peak = jnp.maximum(jnp.max(jnp.abs(block), axis=0, keepdims=True), 1e-30)
    power = jnp.ceil(jnp.log2(peak))
    unit = jnp.exp2(power - 8.0)
    units = jnp.ceil(peak / unit)
    coded = jnp.round(block * (TOP / (units * unit))).astype(jnp.int32)
    return coded.astype(jnp.int16), (power.astype(jnp.int32), units.astype(jnp.int32))


def decode(coded, half, first=0, size=HALF):
    scale = coded[ROWS:].astype(jnp.int32).astype(F32)
    power, units = scale[2 * half : 2 * half + 1], scale[2 * half + 1 : 2 * half + 2]
    step = units * jnp.exp2(power - 8.0) * (1.0 / TOP)
    start = half * HALF + first
    return coded[start : start + size].astype(jnp.int32).astype(F32) * step


def batch_rows(batch):
    return pl.ds(batch * ROWS, ROWS)


def residue_parts(predicted, observed_tile, columns):
    highs, lows = [], []
    for row in range(predicted.shape[0] // TILE):
        high_row, low_row = [], []
        for column in range(columns):
            observed = observed_tile(row, column).astype(F32)
            part = predicted[row * TILE : (row + 1) * TILE, column * TILE : (column + 1) * TILE]
            high, low = split(jnp.where(observed != 0, part - observed, 0.0))
            high_row.append(high)
            low_row.append(low)
        highs.append(jnp.concatenate(high_row, axis=1))
        lows.append(jnp.concatenate(low_row, axis=1))
    return jnp.concatenate(highs, axis=0), jnp.concatenate(lows, axis=0)


def user_piece(parts, piece):
    size = ROWS // PIECES
    return tuple(which[piece * size : (piece + 1) * size] for which in parts)


ORDER = tuple(
    (kind, half, batch) for batch in range(BATCHES) for kind in "PRG" for half in range(HALVES)
)


def block_steps(observed_tile, users_of, halves, blocks_out, before=None):
    parts, predicted, residues = {}, {}, {}
    columns = SIDE // HALVES
    for kind, half, batch in ORDER:
        span = pl.ds(half * HALF, HALF)
        if before is not None:
            before(kind, half, batch)
        if kind == "P":
            parts[half] = split(halves[half])
            for which in range(2):
                blocks_out[batch, which, span] = parts[half][which]
            predicted[half] = [
                product(user_piece(users_of(batch), piece), parts[half], ((1,), (1,)))
                for piece in range(PIECES)
            ]
        elif kind == "R":
            residues[half] = [
                residue_parts(
                    predicted[half][piece],
                    lambda row, column: observed_tile(
                        batch, (row + piece * (SIDE // PIECES)) * SIDE + half * columns + column
                    ),
                    columns,
                )
                for piece in range(PIECES)
            ]
        else:
            whole = tuple(jnp.concatenate(which, axis=0) for which in zip(*residues[half]))
            grad_items = product(whole, users_of(batch), ((0,), (0,)))
            halves[half] = halves[half] - LEARN * (grad_items + DECAY * halves[half])


def users_step(old, parts, block, observed_tile):
    predicted = product(parts, block, ((1,), (1,)))
    residues = residue_parts(
        predicted, lambda row, column: observed_tile(row * SIDE + column), SIDE
    )
    grad_users = product(residues, block, ((1,), (0,)))
    return old - LEARN * (grad_users + DECAY * old)


def store_coded(halves, items_out):
    row = lax.broadcasted_iota(jnp.int32, (EXTRA, RANK), 0)
    scales = jnp.zeros((EXTRA, RANK), jnp.int32)
    for half in range(HALVES):
        coded, scale = encode(halves[half])
        items_out[half * HALF : (half + 1) * HALF] = coded
        for which in range(2):
            scales = jnp.where(row == 2 * half + which, scale[which], scales)
    items_out[ROWS:] = scales.astype(jnp.int16)


def place_slots(where, lists, counts, visit, first, none):
    for batch in range(BATCHES):
        entry = visit * BATCHES + batch
        base = (first + batch) * (PLACES + 1)
        count = counts[entry]
        for place in range(PLACES):
            where[base + place] = none
        for slot in range(SLOTS):
            row = jnp.clip(lists[entry, 0, slot], 0, SIDE - 1)
            column = jnp.clip(lists[entry, 1, slot], 0, SIDE - 1)
            target = jnp.where(slot < count, row * SIDE + column, PLACES)
            where[base + target] = (first + batch) * SLOTS + slot


def fetch_lists(lists_in, counts_in, lists, counts, sems):
    copies = (
        pltpu.make_async_copy(lists_in, lists, sems.at[0]),
        pltpu.make_async_copy(counts_in, counts, sems.at[1]),
    )
    for copy in copies:
        copy.start()
    return copies


def fetch_tiles(ratings_in, tiles, visit, batch, sem):
    slots = pl.ds((visit * BATCHES + batch) * SLOTS, SLOTS)
    copy = pltpu.make_async_copy(ratings_in.at[slots], tiles.at[slots], sem)
    copy.start()
    return copy


def first_block_kernel(
    lists_in, counts_in, users_in, items_in, ratings_in,
    users, items_out, blocks_out,
    items, tiles, lists, counts, where, sems,
):
    list_copies = fetch_lists(lists_in, counts_in, lists, counts, sems)
    copies = []

    def pieces(source, target, first, size, count):
        for piece in range(count):
            rows = pl.ds(first + piece * (size // count), size // count)
            copies.append(
                pltpu.make_async_copy(source.at[rows], target.at[rows], sems.at[2 + len(copies)])
            )
            copies[-1].start()

    pieces(items_in, items, 0, ROWS, 1)
    waits = []
    for batch in range(BATCHES):
        pieces(users_in, users, batch * ROWS, ROWS, 1)
        pieces(ratings_in, tiles, batch * SLOTS, SLOTS, 1)
        waits.append(len(copies))
    tiles[LISTED] = jnp.zeros((TILE, TILE), BF16)
    for copy in list_copies:
        copy.wait()
    place_slots(where, lists, counts, 0, 0, LISTED)
    halves = [None] * HALVES
    user_parts = {}

    def users_of(batch):
        if batch not in user_parts:
            user_parts[batch] = split(users[batch_rows(batch)])
        return user_parts[batch]

    def before(kind, half, batch):
        if kind == "P" and half == 0 and batch == 0:
            for copy in copies[: waits[0] - 1]:
                copy.wait()
        if kind == "P" and batch == 0:
            halves[half] = items[half * HALF : (half + 1) * HALF]
        if kind == "R" and half == 0 and batch == 0:
            for copy in copies[waits[0] - 1 :]:
                copy.wait()

    block_steps(
        lambda batch, place: tiles[where[batch * (PLACES + 1) + place]],
        users_of,
        halves,
        blocks_out,
        before,
    )
    store_coded(halves, items_out)


def first_users_kernel(
    lists_in, counts_in, ratings_in, users, blocks,
    users_out, parts_out, later_out,
    tiles, lists, counts, where, sems,
):
    list_copies = fetch_lists(lists_in, counts_in, lists, counts, sems)
    tile_copies = [
        fetch_tiles(ratings_in, tiles, visit, batch, sems.at[2 + visit * BATCHES + batch])
        for visit in range(VISITS)
        for batch in range(BATCHES)
    ]
    tiles[NONE] = jnp.zeros((TILE, TILE), BF16)
    for copy in list_copies + tuple(tile_copies):
        copy.wait()
    for visit in range(VISITS):
        place_slots(where, lists, counts, visit, visit * BATCHES, NONE)
    for batch in range(BATCHES):
        rows = batch_rows(batch)
        old = users[rows]
        new = users_step(
            old,
            split(old),
            (blocks[batch, 0], blocks[batch, 1]),
            lambda place: tiles[where[batch * (PLACES + 1) + place]],
        )
        users_out[rows] = new
        parts_out[0, rows], parts_out[1, rows] = split(new)
    for batch in range(BATCHES):
        for place in range(PLACES):
            slot = where[(BATCHES + batch) * (PLACES + 1) + place]
            later_out[batch * PLACES + place] = tiles[slot]


def second_block_kernel(parts, items_in, later, items_out, blocks_out):
    halves = [decode(items_in, half) for half in range(HALVES)]
    block_steps(
        lambda batch, place: later[batch * PLACES + place],
        lambda batch: (parts[0, batch_rows(batch)], parts[1, batch_rows(batch)]),
        halves,
        blocks_out,
    )
    store_coded(halves, items_out)


def second_users_kernel(users, parts, blocks, later, users_out, fresh, sems):
    copies = []
    for batch in range(BATCHES):
        rows = batch_rows(batch)
        fresh[rows] = users_step(
            users[rows],
            (parts[0, rows], parts[1, rows]),
            (blocks[batch, 0], blocks[batch, 1]),
            lambda place: later[batch * PLACES + place],
        )
        copies.append(
            pltpu.make_async_copy(fresh.at[rows], users_out.at[rows], sems.at[batch])
        )
        copies[-1].start()
    for copy in copies:
        copy.wait()


def held(value):
    return pltpu.with_memory_space_constraint(value, pltpu.HBM)


SPEC_HBM = pl.BlockSpec(memory_space=pltpu.HBM)
SPEC_VMEM = pl.BlockSpec(memory_space=pltpu.VMEM)
CODED_SHAPE = jax.ShapeDtypeStruct((ROWS + EXTRA, RANK), jnp.int16)
USERS_SHAPE = jax.ShapeDtypeStruct((BATCHES * ROWS, RANK), F32)
PARTS_SHAPE = jax.ShapeDtypeStruct((2, BATCHES * ROWS, RANK), BF16)
LATER_SHAPE = jax.ShapeDtypeStruct((BATCHES * PLACES, TILE, TILE), BF16)
BLOCKS_SHAPE = jax.ShapeDtypeStruct((BATCHES, 2, ROWS, RANK), BF16)
PRODUCT_FLOPS = 2 * 3 * BATCHES * ROWS * ROWS * RANK


def call(kernel, name, outs, out_specs, in_specs, scratch, products, args):
    return pl.pallas_call(
        kernel,
        out_shape=outs,
        in_specs=in_specs,
        out_specs=out_specs,
        scratch_shapes=scratch,
        compiler_params=pltpu.CompilerParams(vmem_limit_bytes=28 * 1024 * 1024),
        cost_estimate=pl.CostEstimate(
            flops=products * PRODUCT_FLOPS, bytes_accessed=1 << 20, transcendentals=0
        ),
        name=name,
    )(*args)


def list_scratch(visits):
    return [
        pltpu.VMEM((visits * LISTED + 1, TILE, TILE), BF16),
        pltpu.SMEM((ENTRIES, 2, SLOTS), jnp.int32),
        pltpu.SMEM((ENTRIES,), jnp.int32),
        pltpu.SMEM((visits * BATCHES * (PLACES + 1),), jnp.int32),
    ]


def first_block(lists, counts, users, items, ratings):
    return call(
        first_block_kernel,
        "first_block",
        (USERS_SHAPE, CODED_SHAPE, BLOCKS_SHAPE),
        (SPEC_VMEM,) * 3,
        [SPEC_HBM] * 5,
        [pltpu.VMEM((ROWS, RANK), F32), *list_scratch(1), pltpu.SemaphoreType.DMA((7,))],
        2,
        (held(lists), held(counts), held(users), held(items), held(ratings)),
    )


def first_users(lists, counts, ratings, users, blocks):
    return call(
        first_users_kernel,
        "first_users",
        (USERS_SHAPE, PARTS_SHAPE, LATER_SHAPE),
        (SPEC_VMEM,) * 3,
        [SPEC_HBM] * 3 + [SPEC_VMEM] * 2,
        [*list_scratch(VISITS), pltpu.SemaphoreType.DMA((2 + ENTRIES,))],
        2,
        (held(lists), held(counts), held(ratings), users, blocks),
    )


def second_block(parts, items, later):
    return call(
        second_block_kernel,
        "second_block",
        (CODED_SHAPE, BLOCKS_SHAPE),
        (SPEC_VMEM,) * 2,
        [SPEC_VMEM] * 3,
        [],
        2,
        (parts, items, later),
    )


def second_users(users, parts, blocks, later):
    return call(
        second_users_kernel,
        "second_users",
        USERS_SHAPE,
        SPEC_HBM,
        [SPEC_VMEM] * 4,
        [pltpu.VMEM((BATCHES * ROWS, RANK), F32), pltpu.SemaphoreType.DMA((BATCHES,))],
        2,
        (users, parts, blocks, later),
    )


PIECE = 128


def unpack_kernel(coded, items_out, items, sems):
    copies = []
    for piece in range(ROWS // PIECE):
        half, first = divmod(piece * PIECE, HALF)
        rows = pl.ds(piece * PIECE, PIECE)
        items[rows] = decode(coded, half, first, PIECE)
        copies.append(pltpu.make_async_copy(items.at[rows], items_out.at[rows], sems.at[piece]))
        copies[-1].start()
    for copy in copies:
        copy.wait()


def unpack(coded):
    return pl.pallas_call(
        unpack_kernel,
        out_shape=jax.ShapeDtypeStruct((ROWS, RANK), F32),
        in_specs=[SPEC_VMEM],
        out_specs=SPEC_HBM,
        scratch_shapes=[
            pltpu.VMEM((ROWS, RANK), F32),
            pltpu.SemaphoreType.DMA((ROWS // PIECE,)),
        ],
        compiler_params=pltpu.CompilerParams(vmem_limit_bytes=8 * 1024 * 1024),
        name="unpack",
    )(coded)


def on_device(user_factors, item_factors, ratings, tile_lists, tile_counts):
    users, coded, blocks = first_block(
        tile_lists, tile_counts, user_factors, item_factors, ratings
    )
    arrived = passed_along(coded, "blk", 1)
    users, parts, later = first_users(tile_lists, tile_counts, ratings, users, blocks)
    coded, blocks = second_block(parts, arrived, later)
    returned = passed_along(coded, "blk", -1)
    users = second_users(users, parts, blocks, later)
    items = unpack(returned)
    return (users, items)


def solution(mesh):
    in_specs = (
        P(("grp", "blk"), None),
        P(("grp", "blk"), None),
        P(("grp", "blk"), None, None),
        P(("grp", "blk"), None, None),
        P(("grp", "blk")),
    )
    out_specs = (P(("grp", "blk"), None), P(("grp", "blk"), None))
    return jax.shard_map(
        on_device, mesh=mesh, in_specs=in_specs, out_specs=out_specs, check_vma=False
    )
```
